128 devices in a mesh: grid: 16 (over z, x_hi, core), pair: 8 (over y, x_lo).
Axes of the slice: x: 4 (x_hi: 2, x_lo: 2; x = x_hi * 2 + x_lo), y: 4, z: 4, core: 2. Of those that a mesh axis runs over, the one named last changes fastest.
Arguments:
- amplitudes: bfloat16 [8, 1500, 1500], P('pair'), may hold values from -6 to 6
- factors: bfloat16 [1500, 6000], P(None, 'grid'), may hold values from -0.15625 to 0.15625
- z_values: bfloat16 [6000, 6000], P('grid', 'pair'), may hold values from -6 to 6
- z_scales: float32 [48, 48], P('grid', 'pair'), may hold values from 0.3 to 3
- pair_index: int32 [8], P('pair'), may hold values from 0 to 11174
- vir_energy: float32 [1500], replicated, may hold values from 0.5 to 2.5
- occ_energy: float32 [150], replicated, may hold values from -4 to -0.5
Outputs:
- update: float32 [8, 2250000], P('pair', 'grid')
The draws below stay inside these ranges and needn't reach their ends.
All inputs are finite; a program needn't handle non-finite values.
Results may differ from the reference program's by a relative error of at most 0.004.
Values may be sent and summed in bfloat16 or wider, within the bound.
No kernel may reach another device: no remote copies, remote signals or barrier semaphores. Data moves between devices by JAX's collectives and lax.ppermute only.
A program may use at most 128 MiB of HBM per device.

```python
import math
import jax
import jax.numpy as jnp
from jax import lax

V = 1500
NOCC = 150
NG = 6000
ZBLK = 125
PAIRS = 8
OCC_PAIRS = 11175


def with_ends(values, stream_key, smallest, largest):
    shape = values.shape
    place = [jax.random.randint(jax.random.fold_in(stream_key, axis), (), 0, shape[axis]) for axis in range(len(shape))]
    values = values.at[tuple(place)].set(smallest)
    longest = shape.index(max(shape))
    place[longest] = (place[longest] + 1) % shape[longest]
    return values.at[tuple(place)].set(largest)


def level_of(key, shape, shards, smallest, largest):
    loudness, own = 1.0, jax.random.fold_in(key, 6)
    for position, parts in shards:
        heights = jnp.exp(jax.random.uniform(jax.random.fold_in(own, position), (parts,), jnp.float32, smallest / len(shards), largest / len(shards)))
        loudness = loudness * jnp.repeat(heights, shape[position] // parts).reshape([-1 if axis == position else 1 for axis in range(len(shape))])
    return loudness


def centred(rng, shape, deviation, limit, cuts=(), held_as=jnp.bfloat16):
    array = jax.random.normal(rng, shape, jnp.float32) * deviation
    if len(cuts) > 0:
        array = level_of(rng, shape, cuts, -0.22, 0.18) * array
    return jnp.clip(array, min=-limit, max=limit).astype(held_as)


def setup_inputs(seed: int = 0) -> dict:
    splits = jax.random.split(jax.random.key(seed), 8)
    return {
        "amplitudes": centred(splits[0], (PAIRS, V, V), 1.0, 6.0, ((0, 8),)),
        "factors": centred(splits[1], (V, NG), V ** -0.5, 0.15625, ((1, 16),)),
        "z_values": centred(splits[2], (NG, NG), 1.0, 6.0, ((0, 16), (1, 8))),
        "z_scales": jnp.clip(jnp.exp(math.log(3.0) - 2.3025851 * jax.random.uniform(splits[3], (NG // ZBLK, NG // ZBLK), jnp.float32) ** level_of(splits[3], (NG // ZBLK, NG // ZBLK), ((0, 16), (1, 8)), -0.2, 0.2)), 0.3, 3.0),
        "pair_index": with_ends(jax.random.randint(splits[4], (PAIRS,), 0, OCC_PAIRS), jax.random.fold_in(splits[4], 1), 0, OCC_PAIRS - 1).astype(jnp.int32),
        "vir_energy": jnp.clip(jax.random.uniform(splits[5], (V,), jnp.float32, 0.5, 2.5), 0.5, 2.5),
        "occ_energy": jnp.clip(jax.random.uniform(splits[6], (NOCC,), jnp.float32, -4.0, -0.5), -4.0, -0.5),
    }


def pair_orbitals(packed, occ_count):
    row_ids = jnp.arange(1, occ_count, dtype=jnp.int32)
    starts = row_ids * (2 * occ_count - row_ids - 1) // 2
    first_occ = jnp.sum((starts[None, :] <= packed[:, None]).astype(jnp.int32), axis=1).astype(jnp.int32)
    second = packed - first_occ * (2 * occ_count - first_occ - 1) // 2 + first_occ + 1
    return first_occ, second.astype(jnp.int32)


def reference(amplitudes, factors, z_values, z_scales, pair_index, vir_energy, occ_energy):
    highest = lax.Precision.HIGHEST
    factors_wide = factors.astype(jnp.float32)
    z_full = z_values.astype(jnp.float32) * jnp.repeat(jnp.repeat(z_scales, ZBLK, axis=0), ZBLK, axis=1)

    def one_pair(single):
        halves = jnp.dot(factors_wide.T, single.astype(jnp.float32), precision=highest).astype(jnp.bfloat16)
        projected = jnp.dot(halves.astype(jnp.float32), factors_wide, precision=highest)
        weighted = (z_full * projected).astype(jnp.bfloat16)
        weighted = lax.optimization_barrier(weighted).astype(jnp.float32)
        back_rows = jnp.dot(weighted, factors_wide.T, precision=highest)
        residual = jnp.dot(factors_wide, back_rows, precision=highest)
        return residual.reshape(V * V)

    residual = lax.map(one_pair, amplitudes)
    first_occ, second_occ = pair_orbitals(pair_index, NOCC)
    occ_sum = occ_energy[first_occ] + occ_energy[second_occ]
    vir_sum = (vir_energy[:, None] + vir_energy[None, :]).reshape(V * V)
    return residual / (vir_sum[None, :] - occ_sum[:, None])
```

```python
import itertools

import jax
import jax.numpy as jnp
from jax import lax
from jax.sharding import PartitionSpec as P

ZBLK = 125
BLK = 375
BPAD = 384
VPAD = 1536
WIN = 96
RING = 4
BOTH = ("grid", "pair")
ALL = list(itertools.product(range(4), range(4), range(2), range(4)))


def flat_index(z, x, c, y):
    return ((z % 4) * 4 + (x % 4) // 2 * 2 + c % 2) * 8 + (y % 4) * 2 + (x % 4) % 2


def move(block, target):
    pairs = []
    for z, x, c, y in ALL:
        dest = target(z, x, c, y)
        if dest is not None:
            pairs.append((flat_index(z, x, c, y), flat_index(*dest)))
    return lax.ppermute(block, BOTH, pairs)


def pair_orbitals(packed, occ_count):
    row_ids = jnp.arange(1, occ_count, dtype=jnp.int32)
    starts = row_ids * (2 * occ_count - row_ids - 1) // 2
    first_occ = jnp.sum((starts[None, :] <= packed[:, None]).astype(jnp.int32), axis=1)
    second = packed - first_occ * (2 * occ_count - first_occ - 1) // 2 + first_occ + 1
    return (first_occ, second)


def dot(a, b, dims):
    return lax.dot_general(a, b, (dims, ((), ())), preferred_element_type=jnp.float32)


def ring_gather(own, axis):
    def shifted(step):
        if axis == "z":
            return lambda z, x, c, y: (z + step, x, c, y)
        return lambda z, x, c, y: (z, x, c, y + step)

    before = move(own, shifted(1))
    after = move(own, shifted(-1))
    half = own.shape[0] // 2
    far_low = move(before[:half], shifted(1))
    far_high = move(after[half:], shifted(-1))
    far = jnp.concatenate([far_low, far_high], axis=0)
    return [own, after, far, before]


def local(amplitudes, factors, z_values, z_scales, pair_index, vir_energy, occ_energy):
    virtuals = factors.shape[0]
    grid_pos = lax.axis_index("grid")
    pair_pos = lax.axis_index("pair")
    z_pos = grid_pos // 4
    x_hi = (grid_pos // 2) % 2
    core = grid_pos % 2
    y_pos = pair_pos // 2
    x_pos = 2 * x_hi + pair_pos % 2
    outer = (x_pos == 0) | (x_pos == 3)

    scales = lax.all_gather(z_scales, BOTH).reshape(16, 8, 3, 6)

    z_own = jnp.pad(z_values, ((0, BPAD - BLK), (0, 2 * (BPAD - BLK))))
    hop_a = {0: 1, 3: 2, 2: 0, 1: 3}
    hop_b = {2: 1, 1: 2}
    recv_a = move(z_own, lambda z, x, c, y: (z, hop_a[x], c, y))
    recv_b = move(z_own, lambda z, x, c, y: (z, hop_b[x], c, y) if x in hop_b else None)
    z_rows = jnp.concatenate(
        [jnp.where(outer, z_own, recv_a), jnp.where(outer, recv_a, recv_b)], axis=0
    )
    z_ring = ring_gather(z_rows, "y")

    x_own = jnp.pad(factors.T, ((0, BPAD - BLK), (0, VPAD - virtuals)))
    x_ring = ring_gather(x_own, "z")
    x_other = move(x_own, lambda z, x, c, y: (z, 3 - x, c, y))
    across = lambda b: move(b, lambda z, x, c, y: (z, x, 1 - c, y))

    p_block = jnp.concatenate([x_own, x_other], axis=0)
    amp = jnp.pad(amplitudes[0], ((0, VPAD - virtuals), (0, VPAD - virtuals)))
    halves = dot(p_block, amp, ((1,), (0,))).astype(jnp.bfloat16)

    z_all = jnp.stack(z_ring)
    back = None
    row_blocks = jnp.stack([z_pos * 4 + x_hi * 2 + core, z_pos * 4 + (1 - x_hi) * 2 + core])
    for step in range(RING):
        mine = x_ring[step]
        theirs = across(mine)
        q_block = jnp.concatenate(
            [jnp.where(core == 0, mine, theirs), jnp.where(core == 0, theirs, mine)], axis=0
        )
        spot = (z_pos + step) % RING
        z_here = lax.dynamic_index_in_dim(z_all, (spot - y_pos) % RING, 0, keepdims=False)
        scale = scales[row_blocks, spot * 2 + x_hi]
        scale = jnp.repeat(jnp.repeat(scale, ZBLK, axis=1), ZBLK, axis=2)
        scale = jnp.pad(scale, ((0, 0), (0, BPAD - BLK), (0, 2 * (BPAD - BLK))))
        scale = scale.reshape(2 * BPAD, 2 * BPAD)
        q_block = jnp.concatenate(
            [q_block[:BLK], q_block[BPAD : BPAD + BLK], jnp.zeros((18, VPAD), q_block.dtype)], axis=0
        )
        projected = dot(halves, q_block, ((1,), (1,)))
        weighted = (projected * (z_here.astype(jnp.float32) * scale)).astype(jnp.bfloat16)
        part = dot(weighted, q_block, ((1,), (0,)))
        back = part if back is None else back + part

    windows = []
    for c in range(2):
        for chip in range(8):
            start = (chip * 2 + c) * BLK // 4
            windows.append(lax.slice_in_dim(p_block, start, start + WIN, axis=1))
    p_windows = jnp.concatenate(windows, axis=1)
    residual = dot(p_windows, back.astype(jnp.bfloat16), ((0,), (0,)))
    residual = residual.reshape(2, 8 * WIN, VPAD)
    keep = lax.dynamic_index_in_dim(residual, core, 0, keepdims=False)
    give = lax.dynamic_index_in_dim(residual, 1 - core, 0, keepdims=False)
    chip_sum = keep + across(give.astype(jnp.bfloat16)).astype(jnp.float32)
    chip_sum = chip_sum.reshape(4, 2, WIN, VPAD)

    def for_dest(dz, dx):
        return lax.dynamic_slice(
            chip_sum, ((z_pos + dz) % 4, (x_hi + dx) % 2, 0, 0), (1, 1, WIN, VPAD)
        )[0, 0]

    total = for_dest(0, 0)
    for dx in range(2):
        for dz in range(4):
            if dx or dz:
                piece = for_dest(dz, dx).astype(jnp.bfloat16)
                total = total + move(
                    piece, lambda z, x, c, y: (z + dz, x + 2 * dx, c, y)
                ).astype(jnp.float32)

    occ_count = occ_energy.shape[0]
    first_occ, second_occ = pair_orbitals(pair_index, occ_count)
    orbital_ids = jnp.arange(occ_count, dtype=jnp.int32)
    one_first = (orbital_ids[None, :] == first_occ[:, None]).astype(jnp.float32)
    one_second = (orbital_ids[None, :] == second_occ[:, None]).astype(jnp.float32)
    occ_sum = jnp.sum((one_first + one_second) * occ_energy[None, :], axis=1)
    share = virtuals * virtuals // 16
    first_row = grid_pos * BLK // 4
    vir_rows = lax.dynamic_slice_in_dim(jnp.pad(vir_energy, (0, VPAD - virtuals)), first_row, WIN, 0)
    out = total[:, :virtuals] / (vir_rows[:, None] + vir_energy[None, :] - occ_sum)
    first_cell = grid_pos * share - first_row * virtuals
    return lax.dynamic_slice_in_dim(out.reshape(1, WIN * virtuals), first_cell, share, 1)


def solution(mesh):
    placed = (
        P("pair", None, None),
        P(None, "grid"),
        P("grid", "pair"),
        P("grid", "pair"),
        P("pair"),
        P(),
        P(),
    )
    return jax.shard_map(
        local, mesh=mesh, in_specs=placed, out_specs=P("pair", "grid"), check_vma=False
    )
```

```python
import itertools

import jax
import jax.numpy as jnp
from jax import lax
from jax.experimental import pallas as pl
from jax.experimental.pallas import tpu as pltpu
from jax.sharding import PartitionSpec as P

VIRT = 1500
ZBLK = 125
BLK = 375
BPAD = 384
TWO = 2 * BPAD
VPAD = 1536
WIN = 96
BOTH = ("grid", "pair")
ALL = list(itertools.product(range(4), range(4), range(2), range(4)))
F32 = jnp.float32
BF16 = jnp.bfloat16


def flat_index(z, x, c, y):
    return ((z % 4) * 4 + (x % 4) // 2 * 2 + c % 2) * 8 + (y % 4) * 2 + (x % 4) % 2


def move(block, target):
    pairs = []
    for z, x, c, y in ALL:
        dest = target(z, x, c, y)
        if dest is not None:
            pairs.append((flat_index(z, x, c, y), flat_index(*dest)))
    return lax.ppermute(block, BOTH, pairs)


def across(block):
    return move(block, lambda z, x, c, y: (z, x, 1 - c, y))


def pair_orbitals(packed, occ_count):
    row_ids = jnp.arange(1, occ_count, dtype=jnp.int32)
    starts = row_ids * (2 * occ_count - row_ids - 1) // 2
    first_occ = jnp.sum((starts[None, :] <= packed[:, None]).astype(jnp.int32), axis=1)
    second = packed - first_occ * (2 * occ_count - first_occ - 1) // 2 + first_occ + 1
    return (first_occ, second)


def dot(a, b, contract_a, contract_b):
    return lax.dot_general(
        a, b, (((contract_a,), (contract_b,)), ((), ())), preferred_element_type=F32
    )


def call(kernel, out_shape, scratch, *args, prefetch=None, aliases=None, grid=(), in_specs=None, out_specs=None):
    vmem = pl.BlockSpec(memory_space=pltpu.VMEM)
    many = isinstance(out_shape, (tuple, list))
    spec = pltpu.PrefetchScalarGridSpec(
        num_scalar_prefetch=0 if prefetch is None else 1,
        grid=grid,
        in_specs=in_specs or [vmem] * len(args),
        out_specs=out_specs or (tuple([vmem] * len(out_shape)) if many else vmem),
        scratch_shapes=scratch,
    )
    lead = () if prefetch is None else (prefetch,)
    return pl.pallas_call(
        kernel,
        out_shape=out_shape,
        grid_spec=spec,
        input_output_aliases=aliases or {},
        compiler_params=pltpu.CompilerParams(vmem_limit_bytes=56 * 2**20),
    )(*lead, *args)


def pad_metric(z_ref, s_ref, o_ref, tmp):
    tmp[...] = jnp.zeros_like(tmp)
    z = z_ref[...].astype(F32)
    tmp[:BLK, :BLK] = z[:, :BLK]
    tmp[:BLK, BPAD : BPAD + BLK] = z[:, BLK:]
    lane = lax.broadcasted_iota(jnp.int32, (1, TWO), 1)
    for r in range(3):
        row = jnp.zeros((1, TWO), F32)
        for q in range(6):
            start = (q // 3) * BPAD + (q % 3) * ZBLK
            row = jnp.where((lane >= start) & (lane < start + ZBLK), s_ref[r, q], row)
        for part in range(3):
            piece = row.astype(BF16).astype(F32)
            tmp[BLK + 3 * part + r : BLK + 3 * part + r + 1, :] = piece
            row = row - piece
    o_ref[...] = tmp[...].astype(BF16)


def scaled(block):
    z = block.astype(F32)
    tail = z[BPAD - 16 :, :]
    parts = [tail[7 + r : 8 + r] + tail[10 + r : 11 + r] + tail[13 + r : 14 + r] for r in range(3)]
    row = lax.broadcasted_iota(jnp.int32, (BPAD, 1), 0)
    scale = jnp.where(row < ZBLK, parts[0], jnp.where(row < 2 * ZBLK, parts[1], parts[2]))
    return jnp.where(row < BLK, z * scale, 0.0)


def pack_factors(info, mine_ref, theirs_ref, *refs):
    o_ref = refs[-1]
    o_ref[...] = jnp.zeros_like(o_ref)

    @pl.when(info[0] == 0)
    def _():
        o_ref[0, :VIRT, :BLK] = mine_ref[...]
        o_ref[0, :VIRT, BPAD : BPAD + BLK] = theirs_ref[...]

    @pl.when(info[0] == 1)
    def _():
        o_ref[0, :VIRT, :BLK] = theirs_ref[...]
        o_ref[0, :VIRT, BPAD : BPAD + BLK] = mine_ref[...]


def first_half(own_ref, other_ref, amp_ref, h_ref, w_ref, xf, tp):
    xf[...] = jnp.zeros_like(xf)
    xf[:VIRT, :BLK] = own_ref[...].astype(F32)
    xf[:VIRT, BPAD : BPAD + BLK] = other_ref[...].astype(F32)
    tp[...] = jnp.zeros_like(tp)
    tp[:VIRT, :VIRT] = amp_ref[0]
    for c in range(2):
        for chip in range(8):
            start = (chip * 2 + c) * BLK // 4
            w_ref[c, chip] = xf[start : start + WIN, :].astype(BF16)
    for r in range(3):
        rows = slice(256 * r, 256 * r + 256)
        left = xf[:, rows].T.astype(BF16)
        h_ref[rows, :] = dot(left, tp[...], 1, 0).astype(BF16)


def ladder(halves, x, zs, rows):
    projected = dot(halves, x, 1, 0)
    weighted = (projected * zs[rows, :]).astype(BF16)
    return dot(weighted, x, 1, 1)


def early_blocks(info, h_ref, x_ref, z0_ref, z1_ref, z2_ref, back_ref, zs):
    step = pl.program_id(0)
    for i, z_ref in enumerate((z0_ref, z1_ref, z2_ref)):

        @pl.when(step == i)
        def _():
            for b in range(2):
                zs[b * BPAD : (b + 1) * BPAD, :] = scaled(z_ref[b])

    for r in range(3):
        rows = slice(256 * r, 256 * r + 256)
        part = ladder(h_ref[rows, :], x_ref[0], zs, rows)

        @pl.when(step == 0)
        def _():
            back_ref[rows, :] = part

        @pl.when(step > 0)
        def _():
            back_ref[rows, :] += part


def last_block(info, h_ref, x_ref, z_ref, back_ref, w_ref, keep_ref, give_ref, zs, bb, left):
    for b in range(2):
        zs[b * BPAD : (b + 1) * BPAD, :] = scaled(z_ref[b])
    for r in range(3):
        rows = slice(256 * r, 256 * r + 256)
        part = ladder(h_ref[rows, :], x_ref[0], zs, rows)
        bb[rows, :] = (back_ref[rows, :] + part).astype(BF16)
    core = info[0]
    for side, o_ref in ((1 - core, give_ref), (core, keep_ref)):
        for j in range(8):
            left[WIN * j : WIN * j + WIN, :] = w_ref[side, info[8 + j]]
        for n in range(6):
            cols = slice(256 * n, 256 * n + 256)
            o_ref[:, cols] = dot(left[...], bb[:, cols], 1, 0).astype(o_ref.dtype)


def chip_total(keep_ref, got_ref, own_ref, *out_refs):
    own_ref[...] = keep_ref[:WIN, :] + got_ref[:WIN, :].astype(F32)
    for j, o_ref in enumerate(out_refs):
        rows = slice(WIN * (j + 1), WIN * (j + 2))
        o_ref[...] = (keep_ref[rows, :] + got_ref[rows, :].astype(F32)).astype(BF16)


def shape(*dims, dtype=BF16):
    return jax.ShapeDtypeStruct(dims, dtype)


def local(amplitudes, factors, z_values, z_scales, pair_index, vir_energy, occ_energy):
    grid_pos = lax.axis_index("grid")
    pair_pos = lax.axis_index("pair")
    z_pos = grid_pos // 4
    x_hi = (grid_pos // 2) % 2
    core = grid_pos % 2
    y_pos = pair_pos // 2
    x_pos = 2 * x_hi + pair_pos % 2
    outer = (x_pos == 0) | (x_pos == 3)
    order = [(y_pos + i) % 4 for i in (0, 1, 3, 2)]
    chips = [(z_pos + j % 4) % 4 * 2 + (x_hi + j // 4) % 2 for j in range(8)]
    info = jnp.stack([core, z_pos, z_pos, z_pos] + order + chips).astype(jnp.int32)

    vmem = pl.BlockSpec(memory_space=pltpu.VMEM)
    z_own = call(
        pad_metric,
        shape(BPAD, TWO),
        [pltpu.VMEM((BPAD, TWO), F32)],
        z_values,
        z_scales,
        in_specs=[vmem, pl.BlockSpec(memory_space=pltpu.SMEM)],
    )
    hop_a = {0: 1, 3: 2, 2: 0, 1: 3}
    hop_b = {2: 1, 1: 2}
    recv_a = move(z_own, lambda z, x, c, y: (z, hop_a[x], c, y))
    recv_b = move(z_own, lambda z, x, c, y: (z, hop_b[x], c, y) if x in hop_b else None)
    z_here = jnp.stack([jnp.where(outer, z_own, recv_a), jnp.where(outer, recv_a, recv_b)])
    z_before = move(z_here, lambda z, x, c, y: (z, x, c, y + 1))
    z_after = move(z_here, lambda z, x, c, y: (z, x, c, y - 1))
    onward = lambda z, x, c, y: (z, x, c, y + 1 - 2 * c)
    z_far = move(jnp.where(core == 0, z_before, z_after), onward)

    x_before = move(factors, lambda z, x, c, y: (z + 1, x, c, y))
    x_after = move(factors, lambda z, x, c, y: (z - 1, x, c, y))
    onward_z = lambda z, x, c, y: (z + 1 - 2 * c, x, c, y)
    x_far = move(jnp.where(core == 0, x_before, x_after), onward_z)
    x_other = move(factors, lambda z, x, c, y: (z, 3 - x, c, y))

    x_all = None
    for step, mine in ((0, factors), (1, x_after), (3, x_before), (2, x_far)):
        args = [mine, across(mine)] + ([] if x_all is None else [x_all])
        x_all = call(
            pack_factors,
            shape(4, VPAD, TWO),
            [],
            *args,
            prefetch=info,
            aliases={} if x_all is None else {3: 0},
            grid=(1,),
            in_specs=[vmem, vmem] + ([] if x_all is None else [pl.BlockSpec(memory_space=pl.ANY)]),
            out_specs=pl.BlockSpec(
                (1, VPAD, TWO), lambda i, info, step=step: (lax.rem(info[1] + step, 4), 0, 0)
            ),
        )

    halves, windows = call(
        first_half,
        (shape(TWO, VPAD), shape(2, 8, WIN, TWO)),
        [pltpu.VMEM((VPAD, TWO), F32), pltpu.VMEM((VPAD, VPAD), BF16)],
        factors,
        x_other,
        amplitudes,
    )
    back = call(
        early_blocks,
        shape(TWO, VPAD, dtype=F32),
        [pltpu.VMEM((TWO, TWO), F32)],
        halves,
        x_all,
        z_here,
        z_after,
        z_before,
        prefetch=info,
        grid=(3,),
        in_specs=[vmem, pl.BlockSpec((1, VPAD, TWO), lambda i, info: (info[4 + i], 0, 0)), vmem, vmem, vmem],
        out_specs=vmem,
    )
    keep, give = call(
        last_block,
        (shape(8 * WIN, VPAD, dtype=F32), shape(8 * WIN, VPAD)),
        [pltpu.VMEM((TWO, TWO), F32), pltpu.VMEM((TWO, VPAD), BF16), pltpu.VMEM((8 * WIN, TWO), BF16)],
        halves,
        x_all,
        z_far,
        back,
        windows,
        prefetch=info,
        grid=(1,),
        in_specs=[vmem, pl.BlockSpec((1, VPAD, TWO), lambda i, info: (info[7], 0, 0)), vmem, vmem, vmem],
        out_specs=(vmem, vmem),
    )
    got = across(give)
    total, *pieces = call(
        chip_total,
        tuple([shape(WIN, VPAD, dtype=F32)] + [shape(WIN, VPAD)] * 7),
        [],
        keep,
        got,
    )
    for j, piece in enumerate(pieces, start=1):
        dz, dx = j % 4, j // 4
        total = total + move(piece, lambda z, x, c, y: (z + dz, x + 2 * dx, c, y)).astype(F32)

    occ_count = occ_energy.shape[0]
    first_occ, second_occ = pair_orbitals(pair_index, occ_count)
    orbital_ids = jnp.arange(occ_count, dtype=jnp.int32)
    one_first = (orbital_ids[None, :] == first_occ[:, None]).astype(F32)
    one_second = (orbital_ids[None, :] == second_occ[:, None]).astype(F32)
    occ_sum = jnp.sum((one_first + one_second) * occ_energy[None, :], axis=1)
    share = VIRT * VIRT // 16
    first_row = grid_pos * BLK // 4
    vir_rows = lax.dynamic_slice_in_dim(jnp.pad(vir_energy, (0, VPAD - VIRT)), first_row, WIN, 0)
    out = total[:, :VIRT] / (vir_rows[:, None] + vir_energy[None, :] - occ_sum)
    first_cell = grid_pos * share - first_row * VIRT
    return lax.dynamic_slice_in_dim(out.reshape(1, WIN * VIRT), first_cell, share, 1)


def solution(mesh):
    placed = (
        P("pair", None, None),
        P(None, "grid"),
        P("grid", "pair"),
        P("grid", "pair"),
        P("pair"),
        P(),
        P(),
    )
    return jax.shard_map(
        local, mesh=mesh, in_specs=placed, out_specs=P("pair", "grid"), check_vma=False
    )
```

```python
import itertools

import jax
import jax.numpy as jnp
from jax import lax
from jax.experimental import pallas as pl
from jax.experimental.pallas import tpu as pltpu
from jax.sharding import PartitionSpec as P

VIRT = 1500
ZBLK = 125
BLK = 375
BPAD = 384
TWO = 2 * BPAD
VPAD = 1536
WIN = 96
BOTH = ("grid", "pair")
ALL = list(itertools.product(range(4), range(4), range(2), range(4)))
F32 = jnp.float32
BF16 = jnp.bfloat16


def flat_index(z, x, c, y):
    return ((z % 4) * 4 + (x % 4) // 2 * 2 + c % 2) * 8 + (y % 4) * 2 + (x % 4) % 2


def move(block, target):
    pairs = []
    for z, x, c, y in ALL:
        dest = target(z, x, c, y)
        if dest is not None:
            pairs.append((flat_index(z, x, c, y), flat_index(*dest)))
    return lax.ppermute(block, BOTH, pairs)


def across(block):
    return move(block, lambda z, x, c, y: (z, x, 1 - c, y))


def pair_orbitals(packed, occ_count):
    row_ids = jnp.arange(1, occ_count, dtype=jnp.int32)
    starts = row_ids * (2 * occ_count - row_ids - 1) // 2
    first_occ = jnp.sum((starts[None, :] <= packed[:, None]).astype(jnp.int32), axis=1)
    second = packed - first_occ * (2 * occ_count - first_occ - 1) // 2 + first_occ + 1
    return (first_occ, second)


def dot(a, b, contract_a, contract_b):
    return lax.dot_general(
        a, b, (((contract_a,), (contract_b,)), ((), ())), preferred_element_type=F32
    )


VMEM = pl.BlockSpec(memory_space=pltpu.VMEM)
SMEM = pl.BlockSpec(memory_space=pltpu.SMEM)
HBM = pl.BlockSpec(memory_space=pl.ANY)


def call(kernel, out_shape, scratch, *args, in_specs=None, out_specs=None):
    many = isinstance(out_shape, (tuple, list))
    return pl.pallas_call(
        kernel,
        out_shape=out_shape,
        in_specs=in_specs or [VMEM] * len(args),
        out_specs=out_specs or (tuple([VMEM] * len(out_shape)) if many else VMEM),
        scratch_shapes=scratch,
        compiler_params=pltpu.CompilerParams(vmem_limit_bytes=56 * 2**20),
    )(*args)


def prepare(z_ref, s_ref, x_ref, z_out, x_out, tmp):
    tmp[...] = jnp.zeros_like(tmp)
    z = z_ref[...].astype(F32)
    tmp[:BLK, :BLK] = z[:, :BLK]
    tmp[:BLK, BPAD : BPAD + BLK] = z[:, BLK:]
    lane = lax.broadcasted_iota(jnp.int32, (1, TWO), 1)
    for r in range(3):
        row = jnp.zeros((1, TWO), F32)
        for q in range(6):
            start = (q // 3) * BPAD + (q % 3) * ZBLK
            row = jnp.where((lane >= start) & (lane < start + ZBLK), s_ref[r, q], row)
        for part in range(3):
            piece = row.astype(BF16).astype(F32)
            tmp[BLK + 3 * part + r : BLK + 3 * part + r + 1, :] = piece
            row = row - piece
    z_out[...] = tmp[...].astype(BF16)
    x_out[...] = jnp.zeros_like(x_out)
    x_out[:VIRT, :BLK] = x_ref[...]


def scaled(block):
    z = block.astype(F32)
    tail = z[BPAD - 16 :, :]
    parts = [tail[7 + r : 8 + r] + tail[10 + r : 11 + r] + tail[13 + r : 14 + r] for r in range(3)]
    row = lax.broadcasted_iota(jnp.int32, (BPAD, 1), 0)
    scale = jnp.where(row < ZBLK, parts[0], jnp.where(row < 2 * ZBLK, parts[1], parts[2]))
    return jnp.where(row < BLK, z * scale, 0.0)


def half_rows(x_ref, xf, w_ref):
    xf[...] = x_ref[...].astype(F32)
    for c in range(2):
        for chip in range(8):
            start = (chip * 2 + c) * BLK // 4
            w_ref[c, chip] = xf[start : start + WIN, :].astype(BF16)
    return xf[...].T.astype(BF16)


def half_own(x_ref, amp_ref, h_ref, w_ref, t_ref, xf):
    t_ref[...] = jnp.zeros_like(t_ref)
    t_ref[:VIRT, :VIRT] = amp_ref[0]
    h_ref[...] = dot(half_rows(x_ref, xf, w_ref), t_ref[...], 1, 0).astype(BF16)


def half_other(x_ref, t_ref, h_ref, w_ref, xf):
    h_ref[...] = dot(half_rows(x_ref, xf, w_ref), t_ref[...], 1, 0).astype(BF16)


def factor_copies(info, place, x_ref, slot_ref, sems):
    return [
        pltpu.make_async_copy(
            x_ref.at[2 * info[4 + place] + c], slot_ref.at[:, pl.ds(c * BPAD, BPAD)], sems.at[c]
        )
        for c in range(2)
    ]


def ladder(h_ref, x, z):
    projected = dot(h_ref[...], x, 1, 0)
    weighted = (projected * scaled(z)).astype(BF16)
    return dot(weighted, x, 1, 1)


def early_blocks(info, h0_ref, h1_ref, x_ref, *refs):
    z_refs, back_out = refs[:3], refs[3]
    xs, zs, acc, xsem, zsem, osem = refs[4:]
    loads = []
    for i in range(3):
        loads.append(factor_copies(info, i, x_ref, xs.at[i], xsem.at[i]))
        loads[i].append(pltpu.make_async_copy(z_refs[i], zs.at[i], zsem.at[i]))
        for load in loads[i]:
            load.start()
    stores = []
    for i in range(3):
        for load in loads[i]:
            load.wait()
        for b, h_ref in enumerate((h0_ref, h1_ref)):
            rows = pl.ds(b * BPAD, BPAD)
            part = ladder(h_ref, xs[i], zs[i, b])
            acc[rows, :] = part if i == 0 else acc[rows, :] + part
            if i == 2:
                stores.append(pltpu.make_async_copy(acc.at[rows, :], back_out.at[rows, :], osem.at[b]))
                stores[b].start()
    for store in stores:
        store.wait()


def gather_windows(info, side, w0_ref, w1_ref, left):
    for j in range(8):
        for b, w_ref in enumerate((w0_ref, w1_ref)):
            left[WIN * j : WIN * j + WIN, b * BPAD : b * BPAD + BPAD] = w_ref[side, info[8 + j]]


def last_block(info, h0_ref, h1_ref, x_ref, z_ref, back_in, w0_ref, w1_ref, back_out, give_ref, xs, acc, left, xsem, bsem):
    loads = factor_copies(info, 3, x_ref, xs, xsem)
    for load in loads:
        load.start()
    back_load = pltpu.make_async_copy(back_in, acc, bsem)
    back_load.start()
    gather_windows(info, 1 - info[0], w0_ref, w1_ref, left)
    for load in loads:
        load.wait()
    for b, h_ref in enumerate((h0_ref, h1_ref)):
        rows = pl.ds(b * BPAD, BPAD)
        part = ladder(h_ref, xs[...], z_ref[b])
        if b == 0:
            back_load.wait()
        back_out[rows, :] = (acc[rows, :] + part).astype(BF16)
    give_ref[...] = dot(left[...], back_out[...], 1, 0).astype(BF16)


def chip_total(info, back_ref, w0_ref, w1_ref, got_ref, own_ref, *refs):
    out_refs, left = refs[:7], refs[7]
    gather_windows(info, info[0], w0_ref, w1_ref, left)
    for n in range(6):
        cols = slice(256 * n, 256 * n + 256)
        part = dot(left[...], back_ref[:, cols], 1, 0) + got_ref[:, cols].astype(F32)
        own_ref[:, cols] = part[:WIN]
        for j, o_ref in enumerate(out_refs):
            o_ref[:, cols] = part[WIN * (j + 1) : WIN * (j + 2)].astype(BF16)


def shape(*dims, dtype=BF16):
    return jax.ShapeDtypeStruct(dims, dtype)


def local(amplitudes, factors, z_values, z_scales, pair_index, vir_energy, occ_energy):
    grid_pos = lax.axis_index("grid")
    pair_pos = lax.axis_index("pair")
    z_pos = grid_pos // 4
    x_hi = (grid_pos // 2) % 2
    core = grid_pos % 2
    y_pos = pair_pos // 2
    x_pos = 2 * x_hi + pair_pos % 2
    outer = (x_pos == 0) | (x_pos == 3)
    order = [(y_pos + i) % 4 for i in (0, 1, 3, 2)]
    chips = [(z_pos + j % 4) % 4 * 2 + (x_hi + j // 4) % 2 for j in range(8)]
    info = jnp.stack([core, core, core, core] + order + chips).astype(jnp.int32)

    z_own, x_own = call(
        prepare,
        (shape(BPAD, TWO), shape(VPAD, BPAD)),
        [pltpu.VMEM((BPAD, TWO), F32)],
        z_values,
        z_scales,
        factors,
        in_specs=[VMEM, SMEM, VMEM],
    )
    hop_a = {0: 1, 3: 2, 2: 0, 1: 3}
    hop_b = {2: 1, 1: 2}
    recv_a = move(z_own, lambda z, x, c, y: (z, hop_a[x], c, y))
    recv_b = move(z_own, lambda z, x, c, y: (z, hop_b[x], c, y) if x in hop_b else None)
    groups = [[4 * z + 2 * h + c for z in range(4) for c in range(2)] for h in range(2)]
    x_all = lax.all_gather(x_own, "grid", axis_index_groups=groups)
    half_0, wins_0, amp = call(
        half_own,
        (shape(BPAD, VPAD), shape(2, 8, WIN, BPAD), shape(VPAD, VPAD)),
        [pltpu.VMEM((VPAD, BPAD), F32)],
        x_own,
        amplitudes,
    )
    z_here = jnp.stack([jnp.where(outer, z_own, recv_a), jnp.where(outer, recv_a, recv_b)])
    z_here, x_again, half_0 = lax.optimization_barrier((z_here, x_own, half_0))
    z_before = move(z_here, lambda z, x, c, y: (z, x, c, y + 1))
    z_after = move(z_here, lambda z, x, c, y: (z, x, c, y - 1))
    x_other = move(x_again, lambda z, x, c, y: (z, 3 - x, c, y))

    z_onward = jnp.where(core == 0, z_before, z_after)
    z_far = move(z_onward, lambda z, x, c, y: (z, x, c, y + 1 - 2 * c))
    half_1, wins_1 = call(
        half_other,
        (shape(BPAD, VPAD), shape(2, 8, WIN, BPAD)),
        [pltpu.VMEM((VPAD, BPAD), F32)],
        x_other,
        amp,
    )
    back = call(
        early_blocks,
        shape(TWO, VPAD, dtype=F32),
        [
            pltpu.VMEM((3, VPAD, TWO), BF16),
            pltpu.VMEM((3, 2, BPAD, TWO), BF16),
            pltpu.VMEM((TWO, VPAD), F32),
            pltpu.SemaphoreType.DMA((3, 2)),
            pltpu.SemaphoreType.DMA((3,)),
            pltpu.SemaphoreType.DMA((2,)),
        ],
        info,
        half_0,
        half_1,
        x_all,
        z_here,
        z_after,
        z_before,
        in_specs=[SMEM] + [VMEM] * 2 + [HBM] * 4,
        out_specs=HBM,
    )
    back_rows, give = call(
        last_block,
        (shape(TWO, VPAD), shape(8 * WIN, VPAD)),
        [
            pltpu.VMEM((VPAD, TWO), BF16),
            pltpu.VMEM((TWO, VPAD), F32),
            pltpu.VMEM((8 * WIN, TWO), BF16),
            pltpu.SemaphoreType.DMA((2,)),
            pltpu.SemaphoreType.DMA,
        ],
        info,
        half_0,
        half_1,
        x_all,
        z_far,
        back,
        wins_0,
        wins_1,
        in_specs=[SMEM] + [VMEM] * 2 + [HBM] + [VMEM, HBM, VMEM, VMEM],
        out_specs=(VMEM, VMEM),
    )
    got = across(give)
    total, *pieces = call(
        chip_total,
        tuple([shape(WIN, VPAD, dtype=F32)] + [shape(WIN, VPAD)] * 7),
        [pltpu.VMEM((8 * WIN, TWO), BF16)],
        info,
        back_rows,
        wins_0,
        wins_1,
        got,
        in_specs=[SMEM] + [VMEM] * 4,
        out_specs=tuple([VMEM] * 8),
    )
    for j, piece in enumerate(pieces, start=1):
        dz, dx = j % 4, j // 4
        total = total + move(piece, lambda z, x, c, y: (z + dz, x + 2 * dx, c, y)).astype(F32)

    occ_count = occ_energy.shape[0]
    first_occ, second_occ = pair_orbitals(pair_index, occ_count)
    orbital_ids = jnp.arange(occ_count, dtype=jnp.int32)
    one_first = (orbital_ids[None, :] == first_occ[:, None]).astype(F32)
    one_second = (orbital_ids[None, :] == second_occ[:, None]).astype(F32)
    occ_sum = jnp.sum((one_first + one_second) * occ_energy[None, :], axis=1)
    share = VIRT * VIRT // 16
    first_row = grid_pos * BLK // 4
    vir_rows = lax.dynamic_slice_in_dim(jnp.pad(vir_energy, (0, VPAD - VIRT)), first_row, WIN, 0)
    out = total[:, :VIRT] / (vir_rows[:, None] + vir_energy[None, :] - occ_sum)
    first_cell = grid_pos * share - first_row * VIRT
    return lax.dynamic_slice_in_dim(out.reshape(1, WIN * VIRT), first_cell, share, 1)


def solution(mesh):
    placed = (
        P("pair", None, None),
        P(None, "grid"),
        P("grid", "pair"),
        P("grid", "pair"),
        P("pair"),
        P(),
        P(),
    )
    return jax.shard_map(
        local, mesh=mesh, in_specs=placed, out_specs=P("pair", "grid"), check_vma=False
    )
```

```python
import itertools

import jax
import jax.numpy as jnp
from jax import lax
from jax.experimental import pallas as pl
from jax.experimental.pallas import tpu as pltpu
from jax.sharding import PartitionSpec as P

VIRT = 1500
ZBLK = 125
BLK = 375
BPAD = 384
TWO = 2 * BPAD
VPAD = 1536
WIN = 96
BOTH = ("grid", "pair")
ALL = list(itertools.product(range(4), range(4), range(2), range(4)))
F32 = jnp.float32
BF16 = jnp.bfloat16


def flat_index(z, x, c, y):
    return ((z % 4) * 4 + (x % 4) // 2 * 2 + c % 2) * 8 + (y % 4) * 2 + (x % 4) % 2


def move(block, target):
    pairs = []
    for z, x, c, y in ALL:
        dest = target(z, x, c, y)
        if dest is not None:
            pairs.append((flat_index(z, x, c, y), flat_index(*dest)))
    return lax.ppermute(block, BOTH, pairs)


def across(block):
    return move(block, lambda z, x, c, y: (z, x, 1 - c, y))


def pair_orbitals(packed, occ_count):
    row_ids = jnp.arange(1, occ_count, dtype=jnp.int32)
    starts = row_ids * (2 * occ_count - row_ids - 1) // 2
    first_occ = jnp.sum((starts[None, :] <= packed[:, None]).astype(jnp.int32), axis=1)
    second = packed - first_occ * (2 * occ_count - first_occ - 1) // 2 + first_occ + 1
    return (first_occ, second)


def dot(a, b, contract_a, contract_b):
    return lax.dot_general(
        a, b, (((contract_a,), (contract_b,)), ((), ())), preferred_element_type=F32
    )


VMEM = pl.BlockSpec(memory_space=pltpu.VMEM)
SMEM = pl.BlockSpec(memory_space=pltpu.SMEM)
HBM = pl.BlockSpec(memory_space=pl.ANY)


def call(kernel, out_shape, scratch, *args, in_specs=None, out_specs=None, mib=20):
    many = isinstance(out_shape, (tuple, list))
    return pl.pallas_call(
        kernel,
        out_shape=out_shape,
        in_specs=in_specs or [VMEM] * len(args),
        out_specs=out_specs or (tuple([VMEM] * len(out_shape)) if many else VMEM),
        scratch_shapes=scratch,
        compiler_params=pltpu.CompilerParams(vmem_limit_bytes=mib * 2**20),
    )(*args)


def pad_metric(z_hbm, s_ref, z_out, tmp, z_ref, sem):
    load = pltpu.make_async_copy(z_hbm, z_ref, sem)
    load.start()
    tmp[...] = jnp.zeros_like(tmp)
    load.wait()
    z = z_ref[...].astype(F32)
    tmp[:BLK, :BLK] = z[:, :BLK]
    tmp[:BLK, BPAD : BPAD + BLK] = z[:, BLK:]
    lane = lax.broadcasted_iota(jnp.int32, (1, TWO), 1)
    for r in range(3):
        row = jnp.zeros((1, TWO), F32)
        for q in range(6):
            start = (q // 3) * BPAD + (q % 3) * ZBLK
            row = jnp.where((lane >= start) & (lane < start + ZBLK), s_ref[r, q], row)
        for part in range(3):
            piece = row.astype(BF16).astype(F32)
            tmp[BLK + 3 * part + r : BLK + 3 * part + r + 1, :] = piece
            row = row - piece
    z_out[...] = tmp[...].astype(BF16)


def pad_factors(own_ref, pair_ref, both_out, own_out):
    both_out[...] = jnp.zeros_like(both_out)
    both_out[0, :VIRT, :BLK] = own_ref[...]
    both_out[1, :VIRT, :BLK] = pair_ref[...]
    own_out[...] = jnp.zeros_like(own_out)
    own_out[:VIRT, :BLK] = own_ref[...]


def scaled(block):
    z = block.astype(F32)
    tail = z[BPAD - 16 :, :]
    parts = [tail[7 + r : 8 + r] + tail[10 + r : 11 + r] + tail[13 + r : 14 + r] for r in range(3)]
    row = lax.broadcasted_iota(jnp.int32, (BPAD, 1), 0)
    scale = jnp.where(row < ZBLK, parts[0], jnp.where(row < 2 * ZBLK, parts[1], parts[2]))
    return jnp.where(row < BLK, z * scale, 0.0)


def half(info, x_ref, amp_ref, h_ref, w_ref, xf):
    if x_ref.shape != xf.shape:
        xf[...] = jnp.zeros_like(xf)
    xf[: x_ref.shape[0], : x_ref.shape[1]] = x_ref[...].astype(F32)
    for c in range(2):
        for chip in range(8):
            start = (chip * 2 + c) * BLK // 4
            w_ref[info[2 + c], info[8 + chip]] = xf[start : start + WIN, :].astype(BF16)
    h_ref[...] = jnp.zeros_like(h_ref)
    h_ref[:, :VIRT] = dot(xf[...].T.astype(BF16)[:, :VIRT], amp_ref[0], 1, 0).astype(BF16)


def copy_whole(in_ref, o_ref):
    o_ref[...] = in_ref[...]


def choose_rows(info, own_ref, a_ref, b_ref, o_ref):
    @pl.when(info[1] == 1)
    def _():
        o_ref[0] = own_ref[...]
        o_ref[1] = a_ref[...]

    @pl.when(info[1] == 0)
    def _():
        o_ref[0] = a_ref[...]
        o_ref[1] = b_ref[...]


def choose_onward(info, first_ref, second_ref, o_ref):
    @pl.when(info[0] == 0)
    def _():
        o_ref[...] = first_ref[...]

    @pl.when(info[0] == 1)
    def _():
        o_ref[...] = second_ref[...]


class Factors:
    def __init__(self, info, step, x_refs, slot, first_col, sems):
        own, near, swapped, far, far_pair = x_refs
        self.info, self.step, self.sems = info, step, sems
        self.slot, self.first_col = slot, first_col
        self.sources = {
            (0, 0): (own.at[0], own.at[1]),
            (0, 1): (own.at[1], own.at[0]),
            (1, 0): (swapped.at[1], swapped.at[0]),
            (1, 1): (near.at[1], near.at[0]),
            (2, 0): (far, far_pair),
            (2, 1): (far_pair, far),
            (3, 0): (near.at[0], near.at[1]),
            (3, 1): (swapped.at[0], swapped.at[1]),
        }

    def copy(self, ref, side):
        to = self.slot.at[:, pl.ds(self.first_col + side * BPAD, BPAD)]
        return pltpu.make_async_copy(ref, to, self.sems.at[side])

    def start(self):
        for (place, core), refs in self.sources.items():

            @pl.when((self.info[4 + self.step] == place) & (self.info[0] == core))
            def _():
                for side in range(2):
                    self.copy(refs[side], side).start()

    def wait(self):
        for side in range(2):
            self.copy(self.sources[2, 0][side], side).wait()


def weigh(h_ref, x, z):
    return (dot(h_ref[...], x, 1, 0) * scaled(z)).astype(BF16)


def weigh_early(info, h0_ref, h1_ref, *refs):
    x_refs, z_refs, w_out, x_out = refs[:5], refs[5:8], refs[8], refs[9]
    zs, xsem, zsem = refs[10:]
    loads = []
    for i in range(3):
        loads.append(Factors(info, i, x_refs, x_out, i * TWO, xsem.at[i]))
        loads.append(pltpu.make_async_copy(z_refs[i], zs.at[i], zsem.at[i]))
        loads[-2].start()
        loads[-1].start()
    for i in range(3):
        loads[2 * i].wait()
        loads[2 * i + 1].wait()
        cols = slice(i * TWO, i * TWO + TWO)
        for b, h_ref in enumerate((h0_ref, h1_ref)):
            w_out[b * BPAD : b * BPAD + BPAD, cols] = weigh(h_ref, x_out[:, cols], zs[i, b])


def window_loads(side, w0_ref, w1_ref, left, sems):
    loads = [
        pltpu.make_async_copy(w_ref.at[side], left.at[:, :, pl.ds(b * BPAD, BPAD)], sems.at[b])
        for b, w_ref in enumerate((w0_ref, w1_ref))
    ]
    for load in loads:
        load.start()
    return loads


def give_half(left_loads, left, back, give_ref):
    for load in left_loads:
        load.wait()
    give_ref[...] = dot(left[...].reshape(8 * WIN, TWO), back, 1, 0).astype(BF16)


def back_half(rows, w_ref, newest_ref, x_ref, xn_ref):
    part = dot(w_ref[...], x_ref[rows, :], 1, 1) + dot(newest_ref[...], xn_ref[rows, :], 1, 1)
    return part.astype(BF16)


def last_block(info, h0_ref, h1_ref, *refs):
    x_refs, z_ref, w_ref, x_ref, w0_ref, w1_ref = refs[:5], *refs[5:10]
    w_out, xn_out, back_out, give_ref, left, xsem, vsem = refs[10:]
    newest = Factors(info, 3, x_refs, xn_out, 0, xsem)
    newest.start()
    left_loads = window_loads(0, w0_ref, w1_ref, left, vsem)
    newest.wait()
    for b, h_ref in enumerate((h0_ref, h1_ref)):
        w_out[b * BPAD : b * BPAD + BPAD, :] = weigh(h_ref, xn_out[...], z_ref[b])
    back_out[...] = back_half(slice(0, TWO), w_ref, w_out, x_ref, xn_out)
    give_half(left_loads, left, back_out[...], give_ref)


def second_half(w_ref, newest_ref, x_ref, xn_ref, w0_ref, w1_ref, back_out, give_ref, left, vsem):
    left_loads = window_loads(0, w0_ref, w1_ref, left, vsem)
    back_out[...] = back_half(slice(TWO, VPAD), w_ref, newest_ref, x_ref, xn_ref)
    give_half(left_loads, left, back_out[...], give_ref)


def keep_sum(back_ref, w0_ref, w1_ref, got_ref, left, vsem):
    for load in window_loads(1, w0_ref, w1_ref, left, vsem):
        load.wait()
    return dot(left[...].reshape(8 * WIN, TWO), back_ref[...], 1, 0) + got_ref[...].astype(F32)


def keep_x(back_ref, w0_ref, w1_ref, got_ref, own_ref, send_ref, left, vsem):
    total = keep_sum(back_ref, w0_ref, w1_ref, got_ref, left, vsem)
    own_ref[...] = total[: 4 * WIN]
    send_ref[...] = total[4 * WIN :].astype(BF16)


def keep_z(back_ref, w0_ref, w1_ref, got_ref, own_ref, *refs):
    send_refs, left, vsem = refs[:3], refs[3], refs[4]
    total = keep_sum(back_ref, w0_ref, w1_ref, got_ref, left, vsem)
    for dx in range(2):
        for dz in range(4):
            part = total[(4 * dx + dz) * WIN : (4 * dx + dz + 1) * WIN]
            if dz == 0:
                own_ref[dx] = part
            else:
                send_refs[dz - 1][dx] = part.astype(BF16)


def then_z(own_ref, got_ref, out_ref, *send_refs):
    total = own_ref[...] + got_ref[...].astype(F32)
    out_ref[...] = total[:WIN]
    for dz in range(1, 4):
        send_refs[dz - 1][...] = total[dz * WIN : (dz + 1) * WIN].astype(BF16)


def then_x(own_ref, got_1, got_2, got_3, out_ref, send_ref):
    total = own_ref[...] + got_1[...].astype(F32) + got_2[...].astype(F32) + got_3[...].astype(F32)
    out_ref[...] = total[0]
    send_ref[...] = total[1].astype(BF16)


def shape(*dims, dtype=BF16):
    return jax.ShapeDtypeStruct(dims, dtype)


def local(amplitudes, factors, z_values, z_scales, pair_index, vir_energy, occ_energy):
    grid_pos = lax.axis_index("grid")
    pair_pos = lax.axis_index("pair")
    z_pos = grid_pos // 4
    x_hi = (grid_pos // 2) % 2
    core = grid_pos % 2
    y_pos = pair_pos // 2
    x_pos = 2 * x_hi + pair_pos % 2
    outer = (x_pos == 0) | (x_pos == 3)
    order = [(y_pos + i - z_pos) % 4 for i in (0, 1, 3, 2)]
    places = [(chip // 2 - z_pos) % 4 + 4 * ((chip % 2 - x_hi) % 2) for chip in range(8)]
    info = jnp.stack([core, outer.astype(jnp.int32), 1 - core, core] + order + places).astype(jnp.int32)

    theirs = across(factors)
    z_own = call(
        pad_metric,
        shape(BPAD, TWO),
        [
            pltpu.VMEM((BPAD, TWO), F32),
            pltpu.VMEM((BLK, 2 * BLK), BF16),
            pltpu.SemaphoreType.DMA,
        ],
        z_values,
        z_scales,
        in_specs=[HBM, SMEM],
        mib=60,
    )
    hop_a = {0: 1, 3: 2, 2: 0, 1: 3}
    hop_b = {2: 1, 1: 2}
    recv_a = move(z_own, lambda z, x, c, y: (z, hop_a[x], c, y))
    recv_b = move(z_own, lambda z, x, c, y: (z, hop_b[x], c, y) if x in hop_b else None)
    theirs, z_own = lax.optimization_barrier((theirs, z_own))
    x_pair, x_own = call(
        pad_factors, (shape(2, VPAD, BPAD), shape(VPAD, BPAD)), [], factors, theirs
    )

    def halves_of(block, amp):
        return call(
            half,
            (shape(BPAD, VPAD), shape(2, 8, WIN, BPAD)),
            [pltpu.VMEM((VPAD, BPAD), F32)],
            info,
            block,
            amp,
            in_specs=[SMEM, VMEM, VMEM],
        )

    half_0, wins_0 = halves_of(x_own, amplitudes)
    onward = lambda z, x, c, y: (z + 1 - 2 * c, x, c, y)
    near = move(x_pair, onward)
    recv_a, recv_b, half_0, x_again, pair_index = lax.optimization_barrier(
        (recv_a, recv_b, half_0, x_own, pair_index)
    )
    x_other = move(x_again, lambda z, x, c, y: (z, 3 - x, c, y))
    z_here = call(
        choose_rows,
        shape(2, BPAD, TWO),
        [],
        info,
        z_own,
        recv_a,
        recv_b,
        in_specs=[SMEM] + [VMEM] * 3,
    )
    z_before = move(z_here, lambda z, x, c, y: (z, x, c, y + 1))
    z_after = move(z_here, lambda z, x, c, y: (z, x, c, y - 1))
    occ_count = occ_energy.shape[0]
    first_occ, second_occ = pair_orbitals(pair_index, occ_count)
    orbital_ids = jnp.arange(occ_count, dtype=jnp.int32)
    one_first = (orbital_ids[None, :] == first_occ[:, None]).astype(F32)
    one_second = (orbital_ids[None, :] == second_occ[:, None]).astype(F32)
    occ_sum = jnp.sum((one_first + one_second) * occ_energy[None, :], axis=1)
    share = VIRT * VIRT // 16
    first_row = grid_pos * BLK // 4
    vir_rows = lax.dynamic_slice_in_dim(jnp.pad(vir_energy, (0, VPAD - VIRT)), first_row, WIN, 0)
    gaps = vir_rows[:, None] + vir_energy[None, :] - occ_sum
    far = move(near[0], onward)
    amp_later, near = lax.optimization_barrier((amplitudes, near))
    amp_again = call(copy_whole, shape(1, VIRT, VIRT), [], amp_later)
    z_before, z_after, near, far, x_other, gaps, amp_again = lax.optimization_barrier(
        (z_before, z_after, near, far, x_other, gaps, amp_again)
    )
    x_parts = [x_pair, near, across(near), far, across(far)]
    z_onward = call(
        choose_onward,
        shape(2, BPAD, TWO),
        [],
        info,
        z_before,
        z_after,
        in_specs=[SMEM] + [VMEM] * 2,
    )
    z_far = move(z_onward, lambda z, x, c, y: (z, x, c, y + 1 - 2 * c))
    half_1, wins_1 = halves_of(x_other, amp_again)
    dma = pltpu.SemaphoreType.DMA
    early, x_early = call(
        weigh_early,
        (shape(TWO, 3 * TWO), shape(VPAD, 3 * TWO)),
        [pltpu.VMEM((3, 2, BPAD, TWO), BF16), dma((3, 2)), dma((3,))],
        info,
        half_0,
        half_1,
        *x_parts,
        z_here,
        z_after,
        z_before,
        in_specs=[SMEM] + [VMEM] * 2 + [HBM] * 8,
    )
    left = pltpu.VMEM((8, WIN, TWO), BF16)
    half_shape = shape(TWO, TWO)
    newest, x_newest, back_a, give_a = call(
        last_block,
        (half_shape, shape(VPAD, TWO), half_shape, half_shape),
        [left, dma((2,)), dma((2,))],
        info,
        half_0,
        half_1,
        *x_parts,
        z_far,
        early,
        x_early,
        wins_0,
        wins_1,
        in_specs=[SMEM] + [VMEM] * 2 + [HBM] * 5 + [VMEM] * 3 + [HBM] * 2,
    )
    got_a = across(give_a)
    back_b, give_b = call(
        second_half,
        (half_shape, half_shape),
        [left, dma((2,))],
        early,
        newest,
        x_early,
        x_newest,
        wins_0,
        wins_1,
        in_specs=[VMEM] * 4 + [HBM] * 2,
    )
    got_b = across(give_b)

    to_z = [None] + [(lambda dz: lambda z, x, c, y: (z + dz, x, c, y))(dz) for dz in range(1, 4)]
    to_x = lambda z, x, c, y: (z, x + 2, c, y)
    own_a, send_a = call(
        keep_x,
        (shape(4 * WIN, TWO, dtype=F32), shape(4 * WIN, TWO)),
        [left, dma((2,))],
        back_a,
        wins_0,
        wins_1,
        got_a,
        in_specs=[VMEM, HBM, HBM, VMEM],
    )
    from_x = move(send_a, to_x)
    own_b, *sends_b = call(
        keep_z,
        tuple([shape(2, WIN, TWO, dtype=F32)] + [shape(2, WIN, TWO)] * 3),
        [left, dma((2,))],
        back_b,
        wins_0,
        wins_1,
        got_b,
        in_specs=[VMEM, HBM, HBM, VMEM],
    )
    from_z = [move(send, to_z[dz]) for dz, send in enumerate(sends_b, start=1)]
    total_a, *sends_a = call(
        then_z, tuple([shape(WIN, TWO, dtype=F32)] + [shape(WIN, TWO)] * 3), [], own_a, from_x
    )
    last_z = [move(send, to_z[dz]) for dz, send in enumerate(sends_a, start=1)]
    total_a, from_z = lax.optimization_barrier((total_a, from_z))
    total_b, send_b = call(
        then_x, (shape(WIN, TWO, dtype=F32), shape(WIN, TWO)), [], own_b, *from_z
    )
    for got in last_z:
        total_a = total_a + got.astype(F32)
    total_b = total_b + move(send_b, to_x).astype(F32)
    total = jnp.concatenate([total_a, total_b], axis=1)

    out = total[:, :VIRT] / gaps
    first_cell = grid_pos * share - first_row * VIRT
    return lax.dynamic_slice_in_dim(out.reshape(1, WIN * VIRT), first_cell, share, 1)


def solution(mesh):
    placed = (
        P("pair", None, None),
        P(None, "grid"),
        P("grid", "pair"),
        P("grid", "pair"),
        P("pair"),
        P(),
        P(),
    )
    return jax.shard_map(
        local, mesh=mesh, in_specs=placed, out_specs=P("pair", "grid"), check_vma=False
    )
```

```python
import itertools

import jax
import jax.numpy as jnp
from jax import lax
from jax.experimental import pallas as pl
from jax.experimental.pallas import tpu as pltpu
from jax.sharding import PartitionSpec as P

VIRT = 1500
ZBLK = 125
BLK = 375
BPAD = 384
TWO = 2 * BPAD
VPAD = 1536
WIN = 96
BOTH = ("grid", "pair")
ALL = list(itertools.product(range(4), range(4), range(2), range(4)))
F32 = jnp.float32
BF16 = jnp.bfloat16


def flat_index(z, x, c, y):
    return ((z % 4) * 4 + (x % 4) // 2 * 2 + c % 2) * 8 + (y % 4) * 2 + (x % 4) % 2


def move(block, target):
    pairs = []
    for z, x, c, y in ALL:
        dest = target(z, x, c, y)
        if dest is not None:
            pairs.append((flat_index(z, x, c, y), flat_index(*dest)))
    return lax.ppermute(block, BOTH, pairs)


def across(block):
    return move(block, lambda z, x, c, y: (z, x, 1 - c, y))


def dot(a, b, contract_a, contract_b):
    return lax.dot_general(
        a, b, (((contract_a,), (contract_b,)), ((), ())), preferred_element_type=F32
    )


VMEM = pl.BlockSpec(memory_space=pltpu.VMEM)
SMEM = pl.BlockSpec(memory_space=pltpu.SMEM)
HBM = pl.BlockSpec(memory_space=pl.ANY)


def call(kernel, out_shape, scratch, *args, in_specs=None, out_specs=None, mib=20, weight=0):
    many = isinstance(out_shape, (tuple, list))
    return pl.pallas_call(
        kernel,
        out_shape=out_shape,
        in_specs=in_specs or [VMEM] * len(args),
        out_specs=out_specs or (tuple([VMEM] * len(out_shape)) if many else VMEM),
        scratch_shapes=scratch,
        cost_estimate=pl.CostEstimate(flops=1 + weight * 10**9, bytes_accessed=1 + weight * 10**6, transcendentals=0),
        compiler_params=pltpu.CompilerParams(vmem_limit_bytes=mib * 2**20),
    )(*args)


def pad_metric(z_hbm, s_ref, z_out, tmp, z_ref, sem):
    load = pltpu.make_async_copy(z_hbm, z_ref, sem)
    load.start()
    tmp[...] = jnp.zeros_like(tmp)
    load.wait()
    z = z_ref[...].astype(F32)
    tmp[:BLK, :BLK] = z[:, :BLK]
    tmp[:BLK, BPAD : BPAD + BLK] = z[:, BLK:]
    lane = lax.broadcasted_iota(jnp.int32, (1, TWO), 1)
    for r in range(3):
        row = jnp.zeros((1, TWO), F32)
        for q in range(6):
            start = (q // 3) * BPAD + (q % 3) * ZBLK
            row = jnp.where((lane >= start) & (lane < start + ZBLK), s_ref[r, q], row)
        for part in range(3):
            piece = row.astype(BF16).astype(F32)
            tmp[BLK + 3 * part + r : BLK + 3 * part + r + 1, :] = piece
            row = row - piece
    z_out[...] = tmp[...].astype(BF16)


def pad_factors(own_ref, pair_ref, both_out, own_out):
    both_out[...] = jnp.zeros_like(both_out)
    both_out[0, :VIRT, :BLK] = own_ref[...]
    both_out[1, :VIRT, :BLK] = pair_ref[...]
    own_out[...] = jnp.zeros_like(own_out)
    own_out[:VIRT, :BLK] = own_ref[...]


def scaled(block):
    z = block.astype(F32)
    tail = z[BPAD - 16 :, :]
    parts = [tail[7 + r : 8 + r] + tail[10 + r : 11 + r] + tail[13 + r : 14 + r] for r in range(3)]
    row = lax.broadcasted_iota(jnp.int32, (BPAD, 1), 0)
    scale = jnp.where(row < ZBLK, parts[0], jnp.where(row < 2 * ZBLK, parts[1], parts[2]))
    return jnp.where(row < BLK, z * scale, 0.0)


def half(info, x_ref, amp_ref, h_ref, w_ref, xf):
    if x_ref.shape != xf.shape:
        xf[...] = jnp.zeros_like(xf)
    xf[: x_ref.shape[0], : x_ref.shape[1]] = x_ref[...].astype(F32)
    for c in range(2):
        for chip in range(8):
            start = (chip * 2 + c) * BLK // 4
            w_ref[info[2 + c], info[8 + chip]] = xf[start : start + WIN, :].astype(BF16)
    h_ref[...] = jnp.zeros_like(h_ref)
    h_ref[:, :VIRT] = dot(xf[...].T.astype(BF16)[:, :VIRT], amp_ref[0], 1, 0).astype(BF16)


def copy_whole(in_ref, o_ref):
    o_ref[...] = in_ref[...]


def choose_rows(info, own_ref, a_ref, b_ref, o_ref):
    @pl.when(info[1] == 1)
    def _():
        o_ref[0] = own_ref[...]
        o_ref[1] = a_ref[...]

    @pl.when(info[1] == 0)
    def _():
        o_ref[0] = a_ref[...]
        o_ref[1] = b_ref[...]


def choose_onward(info, first_ref, second_ref, o_ref):
    @pl.when(info[0] == 0)
    def _():
        o_ref[...] = first_ref[...]

    @pl.when(info[0] == 1)
    def _():
        o_ref[...] = second_ref[...]


class Factors:
    def __init__(self, info, step, x_refs, slot, first_col, sems):
        own, near, swapped, far, far_pair = x_refs
        self.info, self.step, self.sems = info, step, sems
        self.slot, self.first_col = slot, first_col
        self.sources = {
            (0, 0): (own.at[0], own.at[1]),
            (0, 1): (own.at[1], own.at[0]),
            (1, 0): (swapped.at[1], swapped.at[0]),
            (1, 1): (near.at[1], near.at[0]),
            (2, 0): (far, far_pair),
            (2, 1): (far_pair, far),
            (3, 0): (near.at[0], near.at[1]),
            (3, 1): (swapped.at[0], swapped.at[1]),
        }

    def copy(self, ref, side):
        to = self.slot.at[:, pl.ds(self.first_col + side * BPAD, BPAD)]
        return pltpu.make_async_copy(ref, to, self.sems.at[side])

    def start(self):
        for (place, core), refs in self.sources.items():

            @pl.when((self.info[4 + self.step] == place) & (self.info[0] == core))
            def _():
                for side in range(2):
                    self.copy(refs[side], side).start()

    def wait(self):
        for side in range(2):
            self.copy(self.sources[2, 0][side], side).wait()


def weigh(h_ref, x, z):
    return (dot(h_ref[...], x, 1, 0) * scaled(z)).astype(BF16)


def weigh_early(info, h0_ref, h1_ref, *refs):
    x_refs, z_refs, w_out, x_out = refs[:5], refs[5:8], refs[8], refs[9]
    zs, xsem, zsem = refs[10:]
    loads = []
    for i in range(3):
        loads.append(Factors(info, i, x_refs, x_out, i * TWO, xsem.at[i]))
        loads.append(pltpu.make_async_copy(z_refs[i], zs.at[i], zsem.at[i]))
        loads[-2].start()
        loads[-1].start()
    for i in range(3):
        loads[2 * i].wait()
        loads[2 * i + 1].wait()
        cols = slice(i * TWO, i * TWO + TWO)
        for b, h_ref in enumerate((h0_ref, h1_ref)):
            w_out[b * BPAD : b * BPAD + BPAD, cols] = weigh(h_ref, x_out[:, cols], zs[i, b])


def window_loads(side, w0_ref, w1_ref, left, sems):
    loads = [
        pltpu.make_async_copy(w_ref.at[side], left.at[:, :, pl.ds(b * BPAD, BPAD)], sems.at[b])
        for b, w_ref in enumerate((w0_ref, w1_ref))
    ]
    for load in loads:
        load.start()
    return loads


def give_half(left_loads, left, back, give_ref):
    for load in left_loads:
        load.wait()
    give_ref[...] = dot(left[...].reshape(8 * WIN, TWO), back, 1, 0).astype(BF16)


def back_half(rows, w_ref, newest_ref, x_ref, xn_ref):
    part = dot(w_ref[...], x_ref[rows, :], 1, 1) + dot(newest_ref[...], xn_ref[rows, :], 1, 1)
    return part.astype(BF16)


def last_block(info, h0_ref, h1_ref, *refs):
    x_refs, z_ref, w_ref, x_ref, w0_ref, w1_ref = refs[:5], *refs[5:10]
    w_out, xn_out, back_out, give_ref, left, xsem, vsem = refs[10:]
    newest = Factors(info, 3, x_refs, xn_out, 0, xsem)
    newest.start()
    left_loads = window_loads(0, w0_ref, w1_ref, left, vsem)
    newest.wait()
    for b, h_ref in enumerate((h0_ref, h1_ref)):
        w_out[b * BPAD : b * BPAD + BPAD, :] = weigh(h_ref, xn_out[...], z_ref[b])
    back_out[...] = back_half(slice(0, TWO), w_ref, w_out, x_ref, xn_out)
    give_half(left_loads, left, back_out[...], give_ref)


def second_half(w_ref, newest_ref, x_ref, xn_ref, w0_ref, w1_ref, back_out, give_ref, left, vsem):
    left_loads = window_loads(0, w0_ref, w1_ref, left, vsem)
    back_out[...] = back_half(slice(TWO, VPAD), w_ref, newest_ref, x_ref, xn_ref)
    give_half(left_loads, left, back_out[...], give_ref)


def keep_sum(back_ref, w0_ref, w1_ref, got_ref, left, vsem):
    for load in window_loads(1, w0_ref, w1_ref, left, vsem):
        load.wait()
    return dot(left[...].reshape(8 * WIN, TWO), back_ref[...], 1, 0) + got_ref[...].astype(F32)


def keep_x(back_ref, w0_ref, w1_ref, got_ref, own_ref, send_ref, left, vsem):
    total = keep_sum(back_ref, w0_ref, w1_ref, got_ref, left, vsem)
    own_ref[...] = total[: 4 * WIN]
    send_ref[...] = total[4 * WIN :].astype(BF16)


def keep_z(back_ref, w0_ref, w1_ref, got_ref, own_ref, *refs):
    send_refs, left, vsem = refs[:3], refs[3], refs[4]
    total = keep_sum(back_ref, w0_ref, w1_ref, got_ref, left, vsem)
    for dx in range(2):
        for dz in range(4):
            part = total[(4 * dx + dz) * WIN : (4 * dx + dz + 1) * WIN]
            if dz == 0:
                own_ref[dx] = part
            else:
                send_refs[dz - 1][dx] = part.astype(BF16)


def then_z(own_ref, got_ref, out_ref, *send_refs):
    total = own_ref[...] + got_ref[...].astype(F32)
    out_ref[...] = total[:WIN]
    for dz in range(1, 4):
        send_refs[dz - 1][...] = total[dz * WIN : (dz + 1) * WIN].astype(BF16)


def then_x(own_ref, got_1, got_2, got_3, out_ref, send_ref):
    total = own_ref[...] + got_1[...].astype(F32) + got_2[...].astype(F32) + got_3[...].astype(F32)
    out_ref[...] = total[0]
    send_ref[...] = total[1].astype(BF16)


def add_parts(own_ref, *refs):
    o_ref = refs[-1]
    total = own_ref[...]
    for ref in refs[:-1]:
        total = total + ref[...].astype(F32)
    o_ref[...] = total


def finish(numbers, occ_ref, vir_ref, a_ref, b_ref, b1_ref, o_ref, out):
    packed, first_row, first_cell = numbers[0], numbers[1], numbers[2]
    count = occ_ref.shape[1]
    orbital = lax.broadcasted_iota(jnp.int32, (1, count), 1)
    starts = orbital * (2 * count - orbital - 1) // 2
    first_occ = jnp.sum(((starts <= packed) & (orbital > 0)).astype(jnp.int32))
    second_occ = packed - first_occ * (2 * count - first_occ - 1) // 2 + first_occ + 1
    occ = jnp.where(orbital == first_occ, occ_ref[...], 0.0)
    occ = occ + jnp.where(orbital == second_occ, occ_ref[...], 0.0)
    row = lax.broadcasted_iota(jnp.int32, (WIN, VIRT), 0) + first_row
    column = lax.broadcasted_iota(jnp.int32, (WIN, VIRT), 1)
    vir = vir_ref[...]
    vir_rows = jnp.sum(jnp.where(row == column, vir, 0.0), axis=1, keepdims=True)
    vir_rows = jnp.where(row[:, :1] < VIRT, vir_rows, 1.0)
    gaps = vir_rows + vir - jnp.sum(occ, axis=1, keepdims=True)
    out[:, :TWO] = a_ref[...] / gaps[:, :TWO]
    total_b = b_ref[...] + b1_ref[...].astype(F32)
    out[:, TWO:] = total_b[:, : VIRT - TWO] / gaps[:, TWO:]
    rows = o_ref.shape[0]
    for shift in range(0, VIRT, BLK):

        @pl.when(first_cell == shift)
        def _():
            if shift == 0:
                o_ref[...] = out[:rows, :]
            else:
                o_ref[:, : VIRT - shift] = out[:rows, shift:]
                o_ref[:, VIRT - shift :] = out[1 : rows + 1, :shift]


def shape(*dims, dtype=BF16):
    return jax.ShapeDtypeStruct(dims, dtype)


def local(amplitudes, factors, z_values, z_scales, pair_index, vir_energy, occ_energy):
    grid_pos = lax.axis_index("grid")
    pair_pos = lax.axis_index("pair")
    z_pos = grid_pos // 4
    x_hi = (grid_pos // 2) % 2
    core = grid_pos % 2
    y_pos = pair_pos // 2
    x_pos = 2 * x_hi + pair_pos % 2
    outer = (x_pos == 0) | (x_pos == 3)
    order = [(y_pos + i - z_pos) % 4 for i in (0, 1, 3, 2)]
    places = [(chip // 2 - z_pos) % 4 + 4 * ((chip % 2 - x_hi) % 2) for chip in range(8)]
    info = jnp.stack([core, outer.astype(jnp.int32), 1 - core, core] + order + places).astype(jnp.int32)

    theirs = across(factors)
    z_own = call(
        pad_metric,
        shape(BPAD, TWO),
        [
            pltpu.VMEM((BPAD, TWO), F32),
            pltpu.VMEM((BLK, 2 * BLK), BF16),
            pltpu.SemaphoreType.DMA,
        ],
        z_values,
        z_scales,
        in_specs=[HBM, SMEM],
        mib=60,
    )
    hop_a = {0: 1, 3: 2, 2: 0, 1: 3}
    hop_b = {2: 1, 1: 2}
    recv_a = move(z_own, lambda z, x, c, y: (z, hop_a[x], c, y))
    recv_b = move(z_own, lambda z, x, c, y: (z, hop_b[x], c, y) if x in hop_b else None)
    theirs, z_own = lax.optimization_barrier((theirs, z_own))
    x_pair, x_own = call(
        pad_factors, (shape(2, VPAD, BPAD), shape(VPAD, BPAD)), [], factors, theirs
    )

    def halves_of(block, amp, weight=0):
        return call(
            half,
            (shape(BPAD, VPAD), shape(2, 8, WIN, BPAD)),
            [pltpu.VMEM((VPAD, BPAD), F32)],
            info,
            block,
            amp,
            in_specs=[SMEM, VMEM, VMEM],
            weight=weight,
        )

    half_0, wins_0 = halves_of(x_own, amplitudes)
    onward = lambda z, x, c, y: (z + 1 - 2 * c, x, c, y)
    near = move(x_pair, onward)
    recv_a, recv_b, half_0, x_again = lax.optimization_barrier((recv_a, recv_b, half_0, x_own))
    x_other = move(x_again, lambda z, x, c, y: (z, 3 - x, c, y))
    z_here = call(
        choose_rows,
        shape(2, BPAD, TWO),
        [],
        info,
        z_own,
        recv_a,
        recv_b,
        in_specs=[SMEM] + [VMEM] * 3,
        weight=20,
    )
    z_before = move(z_here, lambda z, x, c, y: (z, x, c, y + 1))
    z_after = move(z_here, lambda z, x, c, y: (z, x, c, y - 1))
    far = move(near[0], onward)
    amp_later, far_source = lax.optimization_barrier((amplitudes, near))
    amp_again = call(copy_whole, shape(1, VIRT, VIRT), [], amp_later)
    x_other, amp_again = lax.optimization_barrier((x_other, amp_again))
    half_1, wins_1 = halves_of(x_other, amp_again, 10)
    z_before, z_after, half_1 = lax.optimization_barrier((z_before, z_after, half_1))
    z_onward = call(
        choose_onward,
        shape(2, BPAD, TWO),
        [],
        info,
        z_before,
        z_after,
        in_specs=[SMEM] + [VMEM] * 2,
    )
    z_far = move(z_onward, lambda z, x, c, y: (z, x, c, y + 1 - 2 * c))
    far, _ = lax.optimization_barrier((far, z_onward))
    x_parts = [x_pair, near, across(near), far, across(far)]
    dma = pltpu.SemaphoreType.DMA
    early, x_early = call(
        weigh_early,
        (shape(TWO, 3 * TWO), shape(VPAD, 3 * TWO)),
        [pltpu.VMEM((3, 2, BPAD, TWO), BF16), dma((3, 2)), dma((3,))],
        info,
        half_0,
        half_1,
        *x_parts,
        z_here,
        z_after,
        z_before,
        in_specs=[SMEM] + [VMEM] * 2 + [HBM] * 8,
    )
    left = pltpu.VMEM((8, WIN, TWO), BF16)
    half_shape = shape(TWO, TWO)
    newest, x_newest, back_a, give_a = call(
        last_block,
        (half_shape, shape(VPAD, TWO), half_shape, half_shape),
        [left, dma((2,)), dma((2,))],
        info,
        half_0,
        half_1,
        *x_parts,
        z_far,
        early,
        x_early,
        wins_0,
        wins_1,
        in_specs=[SMEM] + [VMEM] * 2 + [HBM] * 5 + [VMEM] * 3 + [HBM] * 2,
    )
    got_a = across(give_a)
    back_b, give_b = call(
        second_half,
        (half_shape, half_shape),
        [left, dma((2,))],
        early,
        newest,
        x_early,
        x_newest,
        wins_0,
        wins_1,
        in_specs=[VMEM] * 4 + [HBM] * 2,
    )
    got_b = across(give_b)

    to_z = [None] + [(lambda dz: lambda z, x, c, y: (z + dz, x, c, y))(dz) for dz in range(1, 4)]
    to_x = lambda z, x, c, y: (z, x + 2, c, y)
    own_a, send_a = call(
        keep_x,
        (shape(4 * WIN, TWO, dtype=F32), shape(4 * WIN, TWO)),
        [left, dma((2,))],
        back_a,
        wins_0,
        wins_1,
        got_a,
        in_specs=[VMEM, HBM, HBM, VMEM],
    )
    from_x = move(send_a, to_x)
    own_b, *sends_b = call(
        keep_z,
        tuple([shape(2, WIN, TWO, dtype=F32)] + [shape(2, WIN, TWO)] * 3),
        [left, dma((2,))],
        back_b,
        wins_0,
        wins_1,
        got_b,
        in_specs=[VMEM, HBM, HBM, VMEM],
    )
    from_z = [move(send, to_z[dz]) for dz, send in enumerate(sends_b, start=1)]
    total_a, *sends_a = call(
        then_z, tuple([shape(WIN, TWO, dtype=F32)] + [shape(WIN, TWO)] * 3), [], own_a, from_x
    )
    last_z = [move(send, to_z[dz]) for dz, send in enumerate(sends_a, start=1)]
    total_a, from_z = lax.optimization_barrier((total_a, from_z))
    total_b, send_b = call(
        then_x, (shape(WIN, TWO, dtype=F32), shape(WIN, TWO)), [], own_b, *from_z
    )
    total_a = call(add_parts, shape(WIN, TWO, dtype=F32), [], total_a, *last_z, weight=10)
    share = VIRT * VIRT // 16
    first_row = grid_pos * BLK // 4
    first_cell = grid_pos * share - first_row * VIRT
    numbers = jnp.stack([pair_index[0], first_row, first_cell]).astype(jnp.int32)
    out = call(
        finish,
        shape(94, VIRT, dtype=F32),
        [pltpu.VMEM((WIN, VIRT), F32)],
        numbers,
        occ_energy.reshape(1, -1),
        vir_energy.reshape(1, -1),
        total_a,
        total_b,
        move(send_b, to_x),
        in_specs=[SMEM] + [VMEM] * 5,
    )
    return out.reshape(1, 94 * VIRT)[:, :share]


def solution(mesh):
    placed = (
        P("pair", None, None),
        P(None, "grid"),
        P("grid", "pair"),
        P("grid", "pair"),
        P("pair"),
        P(),
        P(),
    )
    return jax.shard_map(
        local, mesh=mesh, in_specs=placed, out_specs=P("pair", "grid"), check_vma=False
    )
```

```python
import itertools

import jax
import jax.numpy as jnp
from jax import lax
from jax.experimental import pallas as pl
from jax.experimental.pallas import tpu as pltpu
from jax.sharding import PartitionSpec as P

VIRT = 1500
ZBLK = 125
BLK = 375
BPAD = 384
TWO = 2 * BPAD
VPAD = 1536
WIN = 96
BOTH = ("grid", "pair")
ALL = list(itertools.product(range(4), range(4), range(2), range(4)))
F32 = jnp.float32
BF16 = jnp.bfloat16


def flat_index(z, x, c, y):
    return ((z % 4) * 4 + (x % 4) // 2 * 2 + c % 2) * 8 + (y % 4) * 2 + (x % 4) % 2


def move(block, target):
    pairs = []
    for z, x, c, y in ALL:
        dest = target(z, x, c, y)
        if dest is not None:
            pairs.append((flat_index(z, x, c, y), flat_index(*dest)))
    return lax.ppermute(block, BOTH, pairs)


def across(block):
    return move(block, lambda z, x, c, y: (z, x, 1 - c, y))


def dot(a, b, contract_a, contract_b):
    return lax.dot_general(
        a, b, (((contract_a,), (contract_b,)), ((), ())), preferred_element_type=F32
    )


VMEM = pl.BlockSpec(memory_space=pltpu.VMEM)
SMEM = pl.BlockSpec(memory_space=pltpu.SMEM)
HBM = pl.BlockSpec(memory_space=pl.ANY)


def call(kernel, out_shape, scratch, *args, in_specs=None, out_specs=None, mib=20, weight=0):
    many = isinstance(out_shape, (tuple, list))
    return pl.pallas_call(
        kernel,
        out_shape=out_shape,
        in_specs=in_specs or [VMEM] * len(args),
        out_specs=out_specs or (tuple([VMEM] * len(out_shape)) if many else VMEM),
        scratch_shapes=scratch,
        cost_estimate=pl.CostEstimate(flops=1 + weight * 10**9, bytes_accessed=1 + weight * 10**6, transcendentals=0),
        compiler_params=pltpu.CompilerParams(vmem_limit_bytes=mib * 2**20),
    )(*args)


def pad_metric(z_hbm, s_ref, z_out, tmp, z_ref, sem):
    load = pltpu.make_async_copy(z_hbm, z_ref, sem)
    load.start()
    tmp[...] = jnp.zeros_like(tmp)
    load.wait()
    z = z_ref[...].astype(F32)
    tmp[:BLK, :BLK] = z[:, :BLK]
    tmp[:BLK, BPAD : BPAD + BLK] = z[:, BLK:]
    lane = lax.broadcasted_iota(jnp.int32, (1, TWO), 1)
    for r in range(3):
        row = jnp.zeros((1, TWO), F32)
        for q in range(6):
            start = (q // 3) * BPAD + (q % 3) * ZBLK
            row = jnp.where((lane >= start) & (lane < start + ZBLK), s_ref[r, q], row)
        for part in range(3):
            piece = row.astype(BF16).astype(F32)
            tmp[BLK + 3 * part + r : BLK + 3 * part + r + 1, :] = piece
            row = row - piece
    z_out[...] = tmp[...].astype(BF16)


def pad_factors(own_ref, pair_ref, both_out, own_out):
    both_out[...] = jnp.zeros_like(both_out)
    both_out[0, :VIRT, :BLK] = own_ref[...]
    both_out[1, :VIRT, :BLK] = pair_ref[...]
    own_out[...] = jnp.zeros_like(own_out)
    own_out[:VIRT, :BLK] = own_ref[...]


def scaled(block):
    z = block.astype(F32)
    tail = z[BPAD - 16 :, :]
    parts = [tail[7 + r : 8 + r] + tail[10 + r : 11 + r] + tail[13 + r : 14 + r] for r in range(3)]
    row = lax.broadcasted_iota(jnp.int32, (BPAD, 1), 0)
    scale = jnp.where(row < ZBLK, parts[0], jnp.where(row < 2 * ZBLK, parts[1], parts[2]))
    return jnp.where(row < BLK, z * scale, 0.0)


def half(info, x_ref, amp_ref, h_ref, w_ref, xf):
    if x_ref.shape != xf.shape:
        xf[...] = jnp.zeros_like(xf)
    xf[: x_ref.shape[0], : x_ref.shape[1]] = x_ref[...].astype(F32)
    for c in range(2):
        for chip in range(8):
            start = (chip * 2 + c) * BLK // 4
            w_ref[info[2 + c], info[8 + chip]] = xf[start : start + WIN, :].astype(BF16)
    h_ref[...] = jnp.zeros_like(h_ref)
    h_ref[:, :VIRT] = dot(xf[...].T.astype(BF16)[:, :VIRT], amp_ref[0], 1, 0).astype(BF16)


def copy_whole(in_ref, o_ref):
    o_ref[...] = in_ref[...]


def choose_rows(info, own_ref, a_ref, b_ref, o_ref):
    @pl.when(info[1] == 1)
    def _():
        o_ref[0] = own_ref[...]
        o_ref[1] = a_ref[...]

    @pl.when(info[1] == 0)
    def _():
        o_ref[0] = a_ref[...]
        o_ref[1] = b_ref[...]


def choose_onward(info, first_ref, second_ref, o_ref):
    @pl.when(info[0] == 0)
    def _():
        o_ref[...] = first_ref[...]

    @pl.when(info[0] == 1)
    def _():
        o_ref[...] = second_ref[...]


class Factors:
    def __init__(self, info, step, x_refs, slot, first_col, sems):
        own, near, swapped, far, far_pair = x_refs
        self.info, self.step, self.sems = info, step, sems
        self.slot, self.first_col = slot, first_col
        self.sources = {
            (0, 0): (own.at[0], own.at[1]),
            (0, 1): (own.at[1], own.at[0]),
            (1, 0): (swapped.at[1], swapped.at[0]),
            (1, 1): (near.at[1], near.at[0]),
            (2, 0): (far, far_pair),
            (2, 1): (far_pair, far),
            (3, 0): (near.at[0], near.at[1]),
            (3, 1): (swapped.at[0], swapped.at[1]),
        }

    def copy(self, ref, side):
        to = self.slot.at[:, pl.ds(self.first_col + side * BPAD, BPAD)]
        return pltpu.make_async_copy(ref, to, self.sems.at[side])

    def start(self):
        for (place, core), refs in self.sources.items():

            @pl.when((self.info[4 + self.step] == place) & (self.info[0] == core))
            def _():
                for side in range(2):
                    self.copy(refs[side], side).start()

    def wait(self):
        for side in range(2):
            self.copy(self.sources[2, 0][side], side).wait()


def weigh(h_ref, x, z):
    return (dot(h_ref[...], x, 1, 0) * scaled(z)).astype(BF16)


def early_blocks(info, h0_ref, h1_ref, *refs):
    x_refs, z_refs, back_out = refs[:5], refs[5:8], refs[8]
    xs, zs, xsem, zsem = refs[9:]
    loads = []
    for i in range(3):
        loads.append(Factors(info, i, x_refs, xs.at[i], 0, xsem.at[i]))
        loads.append(pltpu.make_async_copy(z_refs[i], zs.at[i], zsem.at[i]))
        loads[-2].start()
        loads[-1].start()
    for i in range(3):
        loads[2 * i].wait()
        loads[2 * i + 1].wait()
        for b, h_ref in enumerate((h0_ref, h1_ref)):
            rows = slice(b * BPAD, b * BPAD + BPAD)
            part = dot(weigh(h_ref, xs[i], zs[i, b]), xs[i], 1, 1)
            back_out[rows, :] = part if i == 0 else back_out[rows, :] + part


def window_loads(side, w0_ref, w1_ref, left, sems):
    loads = [
        pltpu.make_async_copy(w_ref.at[side], left.at[:, :, pl.ds(b * BPAD, BPAD)], sems.at[b])
        for b, w_ref in enumerate((w0_ref, w1_ref))
    ]
    for load in loads:
        load.start()
    return loads


def give_half(left_loads, left, back, give_ref):
    for load in left_loads:
        load.wait()
    give_ref[...] = dot(left[...].reshape(8 * WIN, TWO), back, 1, 0).astype(BF16)


def last_block(info, h0_ref, h1_ref, *refs):
    x_refs, z_ref, early_ref, w0_ref, w1_ref = refs[:5], *refs[5:9]
    w_out, xn_out, back_out, give_ref, left, xsem, vsem = refs[9:]
    newest = Factors(info, 3, x_refs, xn_out, 0, xsem)
    newest.start()
    left_loads = window_loads(0, w0_ref, w1_ref, left, vsem)
    newest.wait()
    for b, h_ref in enumerate((h0_ref, h1_ref)):
        w_out[b * BPAD : b * BPAD + BPAD, :] = weigh(h_ref, xn_out[...], z_ref[b])
    part = dot(w_out[...], xn_out[:TWO, :], 1, 1)
    back_out[...] = (early_ref[:, :TWO] + part).astype(BF16)
    give_half(left_loads, left, back_out[...], give_ref)


def second_half(early_ref, newest_ref, xn_ref, w0_ref, w1_ref, back_out, give_ref, left, vsem):
    left_loads = window_loads(0, w0_ref, w1_ref, left, vsem)
    part = dot(newest_ref[...], xn_ref[TWO:, :], 1, 1)
    back_out[...] = (early_ref[:, TWO:] + part).astype(BF16)
    give_half(left_loads, left, back_out[...], give_ref)


def keep_sum(back_ref, w0_ref, w1_ref, got_ref, left, vsem):
    for load in window_loads(1, w0_ref, w1_ref, left, vsem):
        load.wait()
    return dot(left[...].reshape(8 * WIN, TWO), back_ref[...], 1, 0) + got_ref[...].astype(F32)


def keep_x(back_ref, w0_ref, w1_ref, got_ref, own_ref, send_ref, left, vsem):
    total = keep_sum(back_ref, w0_ref, w1_ref, got_ref, left, vsem)
    own_ref[...] = total[: 4 * WIN]
    send_ref[...] = total[4 * WIN :].astype(BF16)


def keep_z(back_ref, w0_ref, w1_ref, got_ref, own_ref, *refs):
    send_refs, left, vsem = refs[:3], refs[3], refs[4]
    total = keep_sum(back_ref, w0_ref, w1_ref, got_ref, left, vsem)
    for dx in range(2):
        for dz in range(4):
            part = total[(4 * dx + dz) * WIN : (4 * dx + dz + 1) * WIN]
            if dz == 0:
                own_ref[dx] = part
            else:
                send_refs[dz - 1][dx] = part.astype(BF16)


def then_z(own_ref, got_ref, out_ref, *send_refs):
    total = own_ref[...] + got_ref[...].astype(F32)
    out_ref[...] = total[:WIN]
    for dz in range(1, 4):
        send_refs[dz - 1][...] = total[dz * WIN : (dz + 1) * WIN].astype(BF16)


def then_x(own_ref, got_1, got_2, got_3, out_ref, send_ref):
    total = own_ref[...] + got_1[...].astype(F32) + got_2[...].astype(F32) + got_3[...].astype(F32)
    out_ref[...] = total[0]
    send_ref[...] = total[1].astype(BF16)


def add_parts(own_ref, *refs):
    o_ref = refs[-1]
    total = own_ref[...]
    for ref in refs[:-1]:
        total = total + ref[...].astype(F32)
    o_ref[...] = total


def finish(numbers, occ_ref, vir_ref, a_ref, b_ref, b1_ref, o_ref, out):
    packed, first_row, first_cell = numbers[0], numbers[1], numbers[2]
    count = occ_ref.shape[1]
    orbital = lax.broadcasted_iota(jnp.int32, (1, count), 1)
    starts = orbital * (2 * count - orbital - 1) // 2
    first_occ = jnp.sum(((starts <= packed) & (orbital > 0)).astype(jnp.int32))
    second_occ = packed - first_occ * (2 * count - first_occ - 1) // 2 + first_occ + 1
    occ = jnp.where(orbital == first_occ, occ_ref[...], 0.0)
    occ = occ + jnp.where(orbital == second_occ, occ_ref[...], 0.0)
    row = lax.broadcasted_iota(jnp.int32, (WIN, VIRT), 0) + first_row
    column = lax.broadcasted_iota(jnp.int32, (WIN, VIRT), 1)
    vir = vir_ref[...]
    vir_rows = jnp.sum(jnp.where(row == column, vir, 0.0), axis=1, keepdims=True)
    vir_rows = jnp.where(row[:, :1] < VIRT, vir_rows, 1.0)
    gaps = vir_rows + vir - jnp.sum(occ, axis=1, keepdims=True)
    out[:, :TWO] = a_ref[...] / gaps[:, :TWO]
    total_b = b_ref[...] + b1_ref[...].astype(F32)
    out[:, TWO:] = total_b[:, : VIRT - TWO] / gaps[:, TWO:]
    rows = o_ref.shape[0]
    for shift in range(0, VIRT, BLK):

        @pl.when(first_cell == shift)
        def _():
            if shift == 0:
                o_ref[...] = out[:rows, :]
            else:
                o_ref[:, : VIRT - shift] = out[:rows, shift:]
                o_ref[:, VIRT - shift :] = out[1 : rows + 1, :shift]


def shape(*dims, dtype=BF16):
    return jax.ShapeDtypeStruct(dims, dtype)


def local(amplitudes, factors, z_values, z_scales, pair_index, vir_energy, occ_energy):
    grid_pos = lax.axis_index("grid")
    pair_pos = lax.axis_index("pair")
    z_pos = grid_pos // 4
    x_hi = (grid_pos // 2) % 2
    core = grid_pos % 2
    y_pos = pair_pos // 2
    x_pos = 2 * x_hi + pair_pos % 2
    outer = (x_pos == 0) | (x_pos == 3)
    order = [(y_pos + i - z_pos) % 4 for i in (0, 1, 3, 2)]
    places = [(chip // 2 - z_pos) % 4 + 4 * ((chip % 2 - x_hi) % 2) for chip in range(8)]
    info = jnp.stack([core, outer.astype(jnp.int32), 1 - core, core] + order + places).astype(jnp.int32)

    theirs = across(factors)
    z_own = call(
        pad_metric,
        shape(BPAD, TWO),
        [
            pltpu.VMEM((BPAD, TWO), F32),
            pltpu.VMEM((BLK, 2 * BLK), BF16),
            pltpu.SemaphoreType.DMA,
        ],
        z_values,
        z_scales,
        in_specs=[HBM, SMEM],
        mib=60,
    )
    hop_a = {0: 1, 3: 2, 2: 0, 1: 3}
    hop_b = {2: 1, 1: 2}
    recv_a = move(z_own, lambda z, x, c, y: (z, hop_a[x], c, y))
    recv_b = move(z_own, lambda z, x, c, y: (z, hop_b[x], c, y) if x in hop_b else None)
    theirs, z_own = lax.optimization_barrier((theirs, z_own))
    x_pair, x_own = call(
        pad_factors, (shape(2, VPAD, BPAD), shape(VPAD, BPAD)), [], factors, theirs
    )

    def halves_of(block, amp, weight=0):
        return call(
            half,
            (shape(BPAD, VPAD), shape(2, 8, WIN, BPAD)),
            [pltpu.VMEM((VPAD, BPAD), F32)],
            info,
            block,
            amp,
            in_specs=[SMEM, VMEM, VMEM],
            weight=weight,
        )

    half_0, wins_0 = halves_of(x_own, amplitudes)
    onward = lambda z, x, c, y: (z + 1 - 2 * c, x, c, y)
    near = move(x_pair, onward)
    recv_a, recv_b, half_0, x_again = lax.optimization_barrier((recv_a, recv_b, half_0, x_own))
    x_other = move(x_again, lambda z, x, c, y: (z, 3 - x, c, y))
    z_here = call(
        choose_rows,
        shape(2, BPAD, TWO),
        [],
        info,
        z_own,
        recv_a,
        recv_b,
        in_specs=[SMEM] + [VMEM] * 3,
        weight=20,
    )
    z_before = move(z_here, lambda z, x, c, y: (z, x, c, y + 1))
    z_after = move(z_here, lambda z, x, c, y: (z, x, c, y - 1))
    far = move(near[0], onward)
    amp_later, far_source = lax.optimization_barrier((amplitudes, near))
    amp_again = call(copy_whole, shape(1, VIRT, VIRT), [], amp_later)
    x_other, amp_again = lax.optimization_barrier((x_other, amp_again))
    half_1, wins_1 = halves_of(x_other, amp_again, 10)
    z_before, z_after, half_1 = lax.optimization_barrier((z_before, z_after, half_1))
    z_onward = call(
        choose_onward,
        shape(2, BPAD, TWO),
        [],
        info,
        z_before,
        z_after,
        in_specs=[SMEM] + [VMEM] * 2,
    )
    z_far = move(z_onward, lambda z, x, c, y: (z, x, c, y + 1 - 2 * c))
    far, _ = lax.optimization_barrier((far, z_onward))
    x_parts = [x_pair, near, across(near), far, across(far)]
    dma = pltpu.SemaphoreType.DMA
    early = call(
        early_blocks,
        shape(TWO, VPAD, dtype=F32),
        [
            pltpu.VMEM((3, VPAD, TWO), BF16),
            pltpu.VMEM((3, 2, BPAD, TWO), BF16),
            dma((3, 2)),
            dma((3,)),
        ],
        info,
        half_0,
        half_1,
        *x_parts,
        z_here,
        z_after,
        z_before,
        in_specs=[SMEM] + [VMEM] * 2 + [HBM] * 8,
    )
    left = pltpu.VMEM((8, WIN, TWO), BF16)
    half_shape = shape(TWO, TWO)
    newest, x_newest, back_a, give_a = call(
        last_block,
        (half_shape, shape(VPAD, TWO), half_shape, half_shape),
        [left, dma((2,)), dma((2,))],
        info,
        half_0,
        half_1,
        *x_parts,
        z_far,
        early,
        wins_0,
        wins_1,
        in_specs=[SMEM] + [VMEM] * 2 + [HBM] * 5 + [VMEM] * 2 + [HBM] * 2,
    )
    got_a = across(give_a)
    back_b, give_b = call(
        second_half,
        (half_shape, half_shape),
        [left, dma((2,))],
        early,
        newest,
        x_newest,
        wins_0,
        wins_1,
        in_specs=[VMEM] * 3 + [HBM] * 2,
    )
    got_b = across(give_b)

    to_z = [None] + [(lambda dz: lambda z, x, c, y: (z + dz, x, c, y))(dz) for dz in range(1, 4)]
    to_x = lambda z, x, c, y: (z, x + 2, c, y)
    own_a, send_a = call(
        keep_x,
        (shape(4 * WIN, TWO, dtype=F32), shape(4 * WIN, TWO)),
        [left, dma((2,))],
        back_a,
        wins_0,
        wins_1,
        got_a,
        in_specs=[VMEM, HBM, HBM, VMEM],
    )
    from_x = move(send_a, to_x)
    own_b, *sends_b = call(
        keep_z,
        tuple([shape(2, WIN, TWO, dtype=F32)] + [shape(2, WIN, TWO)] * 3),
        [left, dma((2,))],
        back_b,
        wins_0,
        wins_1,
        got_b,
        in_specs=[VMEM, HBM, HBM, VMEM],
    )
    from_z = [move(send, to_z[dz]) for dz, send in enumerate(sends_b, start=1)]
    total_a, *sends_a = call(
        then_z, tuple([shape(WIN, TWO, dtype=F32)] + [shape(WIN, TWO)] * 3), [], own_a, from_x
    )
    last_z = [move(send, to_z[dz]) for dz, send in enumerate(sends_a, start=1)]
    total_a, from_z = lax.optimization_barrier((total_a, from_z))
    total_b, send_b = call(
        then_x, (shape(WIN, TWO, dtype=F32), shape(WIN, TWO)), [], own_b, *from_z
    )
    total_a = call(add_parts, shape(WIN, TWO, dtype=F32), [], total_a, *last_z, weight=10)
    share = VIRT * VIRT // 16
    first_row = grid_pos * BLK // 4
    first_cell = grid_pos * share - first_row * VIRT
    numbers = jnp.stack([pair_index[0], first_row, first_cell]).astype(jnp.int32)
    out = call(
        finish,
        shape(94, VIRT, dtype=F32),
        [pltpu.VMEM((WIN, VIRT), F32)],
        numbers,
        occ_energy.reshape(1, -1),
        vir_energy.reshape(1, -1),
        total_a,
        total_b,
        move(send_b, to_x),
        in_specs=[SMEM] + [VMEM] * 5,
    )
    return out.reshape(1, 94 * VIRT)[:, :share]


def solution(mesh):
    placed = (
        P("pair", None, None),
        P(None, "grid"),
        P("grid", "pair"),
        P("grid", "pair"),
        P("pair"),
        P(),
        P(),
    )
    return jax.shard_map(
        local, mesh=mesh, in_specs=placed, out_specs=P("pair", "grid"), check_vma=False
    )
```

```python
import itertools

import jax
import jax.numpy as jnp
from jax import lax
from jax.experimental import pallas as pl
from jax.experimental.pallas import tpu as pltpu
from jax.sharding import PartitionSpec as P

VIRT = 1500
ZBLK = 125
BLK = 375
BPAD = 384
TWO = 2 * BPAD
VPAD = 1536
WIN = 96
BOTH = ("grid", "pair")
ALL = list(itertools.product(range(4), range(4), range(2), range(4)))
F32 = jnp.float32
BF16 = jnp.bfloat16


def flat_index(z, x, c, y):
    return ((z % 4) * 4 + (x % 4) // 2 * 2 + c % 2) * 8 + (y % 4) * 2 + (x % 4) % 2


def move(block, target):
    pairs = []
    for z, x, c, y in ALL:
        dest = target(z, x, c, y)
        if dest is not None:
            pairs.append((flat_index(z, x, c, y), flat_index(*dest)))
    return lax.ppermute(block, BOTH, pairs)


def across(block):
    return move(block, lambda z, x, c, y: (z, x, 1 - c, y))


def dot(a, b, contract_a, contract_b):
    return lax.dot_general(
        a, b, (((contract_a,), (contract_b,)), ((), ())), preferred_element_type=F32
    )


VMEM = pl.BlockSpec(memory_space=pltpu.VMEM)
SMEM = pl.BlockSpec(memory_space=pltpu.SMEM)
HBM = pl.BlockSpec(memory_space=pl.ANY)


def call(kernel, out_shape, scratch, *args, in_specs=None, out_specs=None, mib=20, weight=0):
    many = isinstance(out_shape, (tuple, list))
    return pl.pallas_call(
        kernel,
        out_shape=out_shape,
        in_specs=in_specs or [VMEM] * len(args),
        out_specs=out_specs or (tuple([VMEM] * len(out_shape)) if many else VMEM),
        scratch_shapes=scratch,
        cost_estimate=pl.CostEstimate(flops=1 + weight * 10**9, bytes_accessed=1 + weight * 10**6, transcendentals=0),
        compiler_params=pltpu.CompilerParams(vmem_limit_bytes=mib * 2**20),
    )(*args)


def pad_metric(z_hbm, s_ref, z_out, tmp, z_ref, sem):
    load = pltpu.make_async_copy(z_hbm, z_ref, sem)
    load.start()
    tmp[...] = jnp.zeros_like(tmp)
    load.wait()
    z = z_ref[...].astype(F32)
    tmp[:BLK, :BLK] = z[:, :BLK]
    tmp[:BLK, BPAD : BPAD + BLK] = z[:, BLK:]
    lane = lax.broadcasted_iota(jnp.int32, (1, TWO), 1)
    for r in range(3):
        row = jnp.zeros((1, TWO), F32)
        for q in range(6):
            start = (q // 3) * BPAD + (q % 3) * ZBLK
            row = jnp.where((lane >= start) & (lane < start + ZBLK), s_ref[r, q], row)
        for part in range(3):
            piece = row.astype(BF16).astype(F32)
            tmp[BLK + 3 * part + r : BLK + 3 * part + r + 1, :] = piece
            row = row - piece
    z_out[...] = tmp[...].astype(BF16)


def pad_factors(own_ref, pair_ref, both_out, own_out):
    both_out[...] = jnp.zeros_like(both_out)
    both_out[0, :VIRT, :BLK] = own_ref[...]
    both_out[1, :VIRT, :BLK] = pair_ref[...]
    own_out[...] = jnp.zeros_like(own_out)
    own_out[:VIRT, :BLK] = own_ref[...]


def scaled(block):
    z = block.astype(F32)
    tail = z[BPAD - 16 :, :]
    parts = [tail[7 + r : 8 + r] + tail[10 + r : 11 + r] + tail[13 + r : 14 + r] for r in range(3)]
    row = lax.broadcasted_iota(jnp.int32, (BPAD, 1), 0)
    scale = jnp.where(row < ZBLK, parts[0], jnp.where(row < 2 * ZBLK, parts[1], parts[2]))
    return jnp.where(row < BLK, z * scale, 0.0)


def half(info, x_ref, amp_ref, h_ref, w_ref, xf):
    if x_ref.shape != xf.shape:
        xf[...] = jnp.zeros_like(xf)
    xf[: x_ref.shape[0], : x_ref.shape[1]] = x_ref[...].astype(F32)
    for c in range(2):
        for chip in range(8):
            start = (chip * 2 + c) * BLK // 4
            w_ref[info[2 + c], info[8 + chip]] = xf[start : start + WIN, :].astype(BF16)
    h_ref[...] = jnp.zeros_like(h_ref)
    h_ref[:, :VIRT] = dot(xf[...].T.astype(BF16)[:, :VIRT], amp_ref[0], 1, 0).astype(BF16)


def copy_whole(in_ref, o_ref):
    o_ref[...] = in_ref[...]


def choose_rows(info, own_ref, a_ref, b_ref, o_ref):
    @pl.when(info[1] == 1)
    def _():
        o_ref[0] = own_ref[...]
        o_ref[1] = a_ref[...]

    @pl.when(info[1] == 0)
    def _():
        o_ref[0] = a_ref[...]
        o_ref[1] = b_ref[...]


def choose_onward(info, first_ref, second_ref, o_ref):
    @pl.when(info[0] == 0)
    def _():
        o_ref[...] = first_ref[...]

    @pl.when(info[0] == 1)
    def _():
        o_ref[...] = second_ref[...]


class Factors:
    def __init__(self, info, step, x_refs, slot, first_col, sems):
        own, near, swapped, far, far_pair = x_refs
        self.info, self.step, self.sems = info, step, sems
        self.slot, self.first_col = slot, first_col
        self.sources = {
            (0, 0): (own.at[0], own.at[1]),
            (0, 1): (own.at[1], own.at[0]),
            (1, 0): (swapped.at[1], swapped.at[0]),
            (1, 1): (near.at[1], near.at[0]),
            (2, 0): (far, far_pair),
            (2, 1): (far_pair, far),
            (3, 0): (near.at[0], near.at[1]),
            (3, 1): (swapped.at[0], swapped.at[1]),
        }

    def copy(self, ref, side):
        to = self.slot.at[:, pl.ds(self.first_col + side * BPAD, BPAD)]
        return pltpu.make_async_copy(ref, to, self.sems.at[side])

    def start(self):
        for (place, core), refs in self.sources.items():

            @pl.when((self.info[4 + self.step] == place) & (self.info[0] == core))
            def _():
                for side in range(2):
                    self.copy(refs[side], side).start()

    def wait(self):
        for side in range(2):
            self.copy(self.sources[2, 0][side], side).wait()


def weigh(h_ref, x, z):
    return (dot(h_ref[...], x, 1, 0) * scaled(z)).astype(BF16)


def early_blocks(info, h0_ref, h1_ref, *refs):
    x_refs, z_refs, back_out = refs[:5], refs[5:8], refs[8]
    xs, zs, xsem, zsem = refs[9:]
    for i in range(3):
        Factors(info, i, x_refs, xs.at[i], 0, xsem.at[i]).start()
        pltpu.make_async_copy(z_refs[i], zs.at[i], zsem.at[i]).start()
    back_out[...] = jnp.zeros_like(back_out)

    def block(i, carry):
        Factors(info, i, x_refs, xs.at[i], 0, xsem.at[i]).wait()
        pltpu.make_async_copy(z_refs[0], zs.at[i], zsem.at[i]).wait()
        for b, h_ref in enumerate((h0_ref, h1_ref)):
            rows = slice(b * BPAD, b * BPAD + BPAD)
            x = xs[i]
            back_out[rows, :] += dot(weigh(h_ref, x, zs[i, b]), x, 1, 1)
        return carry

    lax.fori_loop(0, 3, block, 0)


def window_loads(side, w0_ref, w1_ref, left, sems):
    loads = [
        pltpu.make_async_copy(w_ref.at[side], left.at[:, :, pl.ds(b * BPAD, BPAD)], sems.at[b])
        for b, w_ref in enumerate((w0_ref, w1_ref))
    ]
    for load in loads:
        load.start()
    return loads


def give_half(left_loads, left, back, give_ref):
    for load in left_loads:
        load.wait()
    give_ref[...] = dot(left[...].reshape(8 * WIN, TWO), back, 1, 0).astype(BF16)


def last_block(info, h0_ref, h1_ref, *refs):
    x_refs, z_ref, early_ref, w0_ref, w1_ref = refs[:5], *refs[5:9]
    w_out, xn_out, back_out, give_ref, left, xsem, vsem = refs[9:]
    newest = Factors(info, 3, x_refs, xn_out, 0, xsem)
    newest.start()
    left_loads = window_loads(0, w0_ref, w1_ref, left, vsem)
    newest.wait()
    for b, h_ref in enumerate((h0_ref, h1_ref)):
        w_out[b * BPAD : b * BPAD + BPAD, :] = weigh(h_ref, xn_out[...], z_ref[b])
    part = dot(w_out[...], xn_out[:TWO, :], 1, 1)
    back_out[...] = (early_ref[:, :TWO] + part).astype(BF16)
    give_half(left_loads, left, back_out[...], give_ref)


def second_half(early_ref, newest_ref, xn_ref, w0_ref, w1_ref, back_out, give_ref, left, vsem):
    left_loads = window_loads(0, w0_ref, w1_ref, left, vsem)
    part = dot(newest_ref[...], xn_ref[TWO:, :], 1, 1)
    back_out[...] = (early_ref[:, TWO:] + part).astype(BF16)
    give_half(left_loads, left, back_out[...], give_ref)


def keep_sum(back_ref, w0_ref, w1_ref, got_ref, left, vsem):
    for load in window_loads(1, w0_ref, w1_ref, left, vsem):
        load.wait()
    return dot(left[...].reshape(8 * WIN, TWO), back_ref[...], 1, 0) + got_ref[...].astype(F32)


def keep_x(back_ref, w0_ref, w1_ref, got_ref, own_ref, send_ref, left, vsem):
    total = keep_sum(back_ref, w0_ref, w1_ref, got_ref, left, vsem)
    own_ref[...] = total[: 4 * WIN]
    send_ref[...] = total[4 * WIN :].astype(BF16)


def keep_z(back_ref, w0_ref, w1_ref, got_ref, own_ref, *refs):
    send_refs, left, vsem = refs[:3], refs[3], refs[4]
    total = keep_sum(back_ref, w0_ref, w1_ref, got_ref, left, vsem)
    for dx in range(2):
        for dz in range(4):
            part = total[(4 * dx + dz) * WIN : (4 * dx + dz + 1) * WIN]
            if dz == 0:
                own_ref[dx] = part
            else:
                send_refs[dz - 1][dx] = part.astype(BF16)


def then_z(own_ref, got_ref, out_ref, *send_refs):
    total = own_ref[...] + got_ref[...].astype(F32)
    out_ref[...] = total[:WIN]
    for dz in range(1, 4):
        send_refs[dz - 1][...] = total[dz * WIN : (dz + 1) * WIN].astype(BF16)


def then_x(own_ref, got_1, got_2, got_3, out_ref, send_ref):
    total = own_ref[...] + got_1[...].astype(F32) + got_2[...].astype(F32) + got_3[...].astype(F32)
    out_ref[...] = total[0]
    send_ref[...] = total[1].astype(BF16)


def add_parts(own_ref, *refs):
    o_ref = refs[-1]
    total = own_ref[...]
    for ref in refs[:-1]:
        total = total + ref[...].astype(F32)
    o_ref[...] = total


def finish(numbers, occ_ref, vir_ref, a_ref, b_ref, b1_ref, o_ref, out):
    packed, first_row, first_cell = numbers[0], numbers[1], numbers[2]
    count = occ_ref.shape[1]
    orbital = lax.broadcasted_iota(jnp.int32, (1, count), 1)
    starts = orbital * (2 * count - orbital - 1) // 2
    first_occ = jnp.sum(((starts <= packed) & (orbital > 0)).astype(jnp.int32))
    second_occ = packed - first_occ * (2 * count - first_occ - 1) // 2 + first_occ + 1
    occ = jnp.where(orbital == first_occ, occ_ref[...], 0.0)
    occ = occ + jnp.where(orbital == second_occ, occ_ref[...], 0.0)
    row = lax.broadcasted_iota(jnp.int32, (WIN, VIRT), 0) + first_row
    column = lax.broadcasted_iota(jnp.int32, (WIN, VIRT), 1)
    vir = vir_ref[...]
    vir_rows = jnp.sum(jnp.where(row == column, vir, 0.0), axis=1, keepdims=True)
    vir_rows = jnp.where(row[:, :1] < VIRT, vir_rows, 1.0)
    gaps = vir_rows + vir - jnp.sum(occ, axis=1, keepdims=True)
    out[:, :TWO] = a_ref[...] / gaps[:, :TWO]
    total_b = b_ref[...] + b1_ref[...].astype(F32)
    out[:, TWO:] = total_b[:, : VIRT - TWO] / gaps[:, TWO:]
    rows = o_ref.shape[0]
    for shift in range(0, VIRT, BLK):

        @pl.when(first_cell == shift)
        def _():
            if shift == 0:
                o_ref[...] = out[:rows, :]
            else:
                o_ref[:, : VIRT - shift] = out[:rows, shift:]
                o_ref[:, VIRT - shift :] = out[1 : rows + 1, :shift]


def shape(*dims, dtype=BF16):
    return jax.ShapeDtypeStruct(dims, dtype)


def local(amplitudes, factors, z_values, z_scales, pair_index, vir_energy, occ_energy):
    grid_pos = lax.axis_index("grid")
    pair_pos = lax.axis_index("pair")
    z_pos = grid_pos // 4
    x_hi = (grid_pos // 2) % 2
    core = grid_pos % 2
    y_pos = pair_pos // 2
    x_pos = 2 * x_hi + pair_pos % 2
    outer = (x_pos == 0) | (x_pos == 3)
    order = [(y_pos + i - z_pos) % 4 for i in (0, 1, 3, 2)]
    places = [(chip // 2 - z_pos) % 4 + 4 * ((chip % 2 - x_hi) % 2) for chip in range(8)]
    info = jnp.stack([core, outer.astype(jnp.int32), 1 - core, core] + order + places).astype(jnp.int32)

    theirs = across(factors)
    z_own = call(
        pad_metric,
        shape(BPAD, TWO),
        [
            pltpu.VMEM((BPAD, TWO), F32),
            pltpu.VMEM((BLK, 2 * BLK), BF16),
            pltpu.SemaphoreType.DMA,
        ],
        z_values,
        z_scales,
        in_specs=[HBM, SMEM],
        mib=60,
    )
    hop_a = {0: 1, 3: 2, 2: 0, 1: 3}
    hop_b = {2: 1, 1: 2}
    recv_a = move(z_own, lambda z, x, c, y: (z, hop_a[x], c, y))
    recv_b = move(z_own, lambda z, x, c, y: (z, hop_b[x], c, y) if x in hop_b else None)
    theirs, z_own = lax.optimization_barrier((theirs, z_own))
    x_pair, x_own = call(
        pad_factors, (shape(2, VPAD, BPAD), shape(VPAD, BPAD)), [], factors, theirs
    )

    def halves_of(block, amp, weight=0):
        return call(
            half,
            (shape(BPAD, VPAD), shape(2, 8, WIN, BPAD)),
            [pltpu.VMEM((VPAD, BPAD), F32)],
            info,
            block,
            amp,
            in_specs=[SMEM, VMEM, VMEM],
            weight=weight,
        )

    half_0, wins_0 = halves_of(x_own, amplitudes)
    onward = lambda z, x, c, y: (z + 1 - 2 * c, x, c, y)
    near = move(x_pair, onward)
    recv_a, recv_b, half_0, x_again = lax.optimization_barrier((recv_a, recv_b, half_0, x_own))
    x_other = move(x_again, lambda z, x, c, y: (z, 3 - x, c, y))
    z_here = call(
        choose_rows,
        shape(2, BPAD, TWO),
        [],
        info,
        z_own,
        recv_a,
        recv_b,
        in_specs=[SMEM] + [VMEM] * 3,
        weight=20,
    )
    z_before = move(z_here, lambda z, x, c, y: (z, x, c, y + 1))
    z_after = move(z_here, lambda z, x, c, y: (z, x, c, y - 1))
    far = move(near[0], onward)
    amp_later, far_source = lax.optimization_barrier((amplitudes, near))
    amp_again = call(copy_whole, shape(1, VIRT, VIRT), [], amp_later)
    x_other, amp_again = lax.optimization_barrier((x_other, amp_again))
    half_1, wins_1 = halves_of(x_other, amp_again, 10)
    z_before, z_after, half_1 = lax.optimization_barrier((z_before, z_after, half_1))
    z_onward = call(
        choose_onward,
        shape(2, BPAD, TWO),
        [],
        info,
        z_before,
        z_after,
        in_specs=[SMEM] + [VMEM] * 2,
    )
    z_far = move(z_onward, lambda z, x, c, y: (z, x, c, y + 1 - 2 * c))
    far, _ = lax.optimization_barrier((far, z_onward))
    x_parts = [x_pair, near, across(near), far, across(far)]
    dma = pltpu.SemaphoreType.DMA
    early = call(
        early_blocks,
        shape(TWO, VPAD, dtype=F32),
        [
            pltpu.VMEM((3, VPAD, TWO), BF16),
            pltpu.VMEM((3, 2, BPAD, TWO), BF16),
            dma((3, 2)),
            dma((3,)),
        ],
        info,
        half_0,
        half_1,
        *x_parts,
        z_here,
        z_after,
        z_before,
        in_specs=[SMEM] + [VMEM] * 2 + [HBM] * 8,
    )
    left = pltpu.VMEM((8, WIN, TWO), BF16)
    half_shape = shape(TWO, TWO)
    newest, x_newest, back_a, give_a = call(
        last_block,
        (half_shape, shape(VPAD, TWO), half_shape, half_shape),
        [left, dma((2,)), dma((2,))],
        info,
        half_0,
        half_1,
        *x_parts,
        z_far,
        early,
        wins_0,
        wins_1,
        in_specs=[SMEM] + [VMEM] * 2 + [HBM] * 5 + [VMEM] * 2 + [HBM] * 2,
    )
    got_a = across(give_a)
    back_b, give_b = call(
        second_half,
        (half_shape, half_shape),
        [left, dma((2,))],
        early,
        newest,
        x_newest,
        wins_0,
        wins_1,
        in_specs=[VMEM] * 3 + [HBM] * 2,
    )
    got_b = across(give_b)

    to_z = [None] + [(lambda dz: lambda z, x, c, y: (z + dz, x, c, y))(dz) for dz in range(1, 4)]
    to_x = lambda z, x, c, y: (z, x + 2, c, y)
    own_a, send_a = call(
        keep_x,
        (shape(4 * WIN, TWO, dtype=F32), shape(4 * WIN, TWO)),
        [left, dma((2,))],
        back_a,
        wins_0,
        wins_1,
        got_a,
        in_specs=[VMEM, HBM, HBM, VMEM],
    )
    from_x = move(send_a, to_x)
    own_b, *sends_b = call(
        keep_z,
        tuple([shape(2, WIN, TWO, dtype=F32)] + [shape(2, WIN, TWO)] * 3),
        [left, dma((2,))],
        back_b,
        wins_0,
        wins_1,
        got_b,
        in_specs=[VMEM, HBM, HBM, VMEM],
    )
    from_z = [move(send, to_z[dz]) for dz, send in enumerate(sends_b, start=1)]
    total_a, *sends_a = call(
        then_z, tuple([shape(WIN, TWO, dtype=F32)] + [shape(WIN, TWO)] * 3), [], own_a, from_x
    )
    last_z = [move(send, to_z[dz]) for dz, send in enumerate(sends_a, start=1)]
    total_a, from_z = lax.optimization_barrier((total_a, from_z))
    total_b, send_b = call(
        then_x, (shape(WIN, TWO, dtype=F32), shape(WIN, TWO)), [], own_b, *from_z
    )
    total_a = call(add_parts, shape(WIN, TWO, dtype=F32), [], total_a, *last_z, weight=10)
    share = VIRT * VIRT // 16
    first_row = grid_pos * BLK // 4
    first_cell = grid_pos * share - first_row * VIRT
    numbers = jnp.stack([pair_index[0], first_row, first_cell]).astype(jnp.int32)
    out = call(
        finish,
        shape(94, VIRT, dtype=F32),
        [pltpu.VMEM((WIN, VIRT), F32)],
        numbers,
        occ_energy.reshape(1, -1),
        vir_energy.reshape(1, -1),
        total_a,
        total_b,
        move(send_b, to_x),
        in_specs=[SMEM] + [VMEM] * 5,
    )
    return out.reshape(1, 94 * VIRT)[:, :share]


def solution(mesh):
    placed = (
        P("pair", None, None),
        P(None, "grid"),
        P("grid", "pair"),
        P("grid", "pair"),
        P("pair"),
        P(),
        P(),
    )
    return jax.shard_map(
        local, mesh=mesh, in_specs=placed, out_specs=P("pair", "grid"), check_vma=False
    )
```

```python
import itertools

import jax
import jax.numpy as jnp
from jax import lax
from jax.experimental import pallas as pl
from jax.experimental.pallas import tpu as pltpu
from jax.sharding import PartitionSpec as P

VIRT = 1500
ZBLK = 125
BLK = 375
BPAD = 384
TWO = 2 * BPAD
VPAD = 1536
WIN = 96
BOTH = ("grid", "pair")
ALL = list(itertools.product(range(4), range(4), range(2), range(4)))
F32 = jnp.float32
BF16 = jnp.bfloat16


def flat_index(z, x, c, y):
    return ((z % 4) * 4 + (x % 4) // 2 * 2 + c % 2) * 8 + (y % 4) * 2 + (x % 4) % 2


def move(block, target):
    pairs = []
    for z, x, c, y in ALL:
        dest = target(z, x, c, y)
        if dest is not None:
            pairs.append((flat_index(z, x, c, y), flat_index(*dest)))
    return lax.ppermute(block, BOTH, pairs)


def across(block):
    return move(block, lambda z, x, c, y: (z, x, 1 - c, y))


def dot(a, b, contract_a, contract_b):
    return lax.dot_general(
        a, b, (((contract_a,), (contract_b,)), ((), ())), preferred_element_type=F32
    )


VMEM = pl.BlockSpec(memory_space=pltpu.VMEM)
SMEM = pl.BlockSpec(memory_space=pltpu.SMEM)
HBM = pl.BlockSpec(memory_space=pl.ANY)


def call(kernel, out_shape, scratch, *args, in_specs=None, out_specs=None, mib=12, weight=0):
    many = isinstance(out_shape, (tuple, list))
    return pl.pallas_call(
        kernel,
        out_shape=out_shape,
        in_specs=in_specs or [VMEM] * len(args),
        out_specs=out_specs or (tuple([VMEM] * len(out_shape)) if many else VMEM),
        scratch_shapes=scratch,
        cost_estimate=pl.CostEstimate(flops=1 + weight * 10**9, bytes_accessed=1 + weight * 10**6, transcendentals=0),
        compiler_params=pltpu.CompilerParams(vmem_limit_bytes=mib * 2**20),
    )(*args)


def pad_metric(z_hbm, s_ref, z_out, tail, z_ref, sem):
    load = pltpu.make_async_copy(z_hbm, z_ref, sem)
    load.start()
    tail[...] = jnp.zeros_like(tail)
    lane = lax.broadcasted_iota(jnp.int32, (1, TWO), 1)
    for r in range(3):
        row = jnp.zeros((1, TWO), F32)
        for q in range(6):
            start = (q // 3) * BPAD + (q % 3) * ZBLK
            row = jnp.where((lane >= start) & (lane < start + ZBLK), s_ref[r, q], row)
        for part in range(3):
            piece = row.astype(BF16).astype(F32)
            tail[7 + 3 * part + r : 8 + 3 * part + r, :] = piece
            row = row - piece
    load.wait()
    top = BPAD - 16
    for half in range(2):
        cols = slice(half * BLK, half * BLK + BLK)
        z_out[:, half * BPAD + 256 : half * BPAD + BPAD] = jnp.zeros((BPAD, 128), BF16)
        z_out[:top, half * BPAD : half * BPAD + BLK] = z_ref[:top, cols]
        tail[:7, half * BPAD : half * BPAD + BLK] = z_ref[top:, cols].astype(F32)
    z_out[top:, :] = tail[...].astype(BF16)


def pad_factors(own_ref, pair_ref, both_out, own_out):
    for out, ref in ((both_out.at[0], own_ref), (both_out.at[1], pair_ref), (own_out, own_ref)):
        out[:, 256:] = jnp.zeros((VPAD, BPAD - 256), BF16)
        out[VIRT - 12 :, :] = jnp.zeros((VPAD - VIRT + 12, BPAD), BF16)
        out[:VIRT, :BLK] = ref[...]


def scaled(block):
    z = block.astype(F32)
    tail = z[BPAD - 16 :, :]
    parts = [tail[7 + r : 8 + r] + tail[10 + r : 11 + r] + tail[13 + r : 14 + r] for r in range(3)]
    row = lax.broadcasted_iota(jnp.int32, (BPAD, 1), 0)
    scale = jnp.where(row < ZBLK, parts[0], jnp.where(row < 2 * ZBLK, parts[1], parts[2]))
    return jnp.where(row < BLK, z * scale, 0.0)


def half(info, x_ref, amp_ref, h_ref, w_ref, xf):
    if x_ref.shape != xf.shape:
        xf[...] = jnp.zeros_like(xf)
    xf[: x_ref.shape[0], : x_ref.shape[1]] = x_ref[...].astype(F32)
    for c in range(2):
        for chip in range(8):
            start = (chip * 2 + c) * BLK // 4
            w_ref[info[2 + c], info[8 + chip]] = xf[start : start + WIN, :].astype(BF16)
    h_ref[...] = jnp.zeros_like(h_ref)
    h_ref[:, :VIRT] = dot(xf[...].T.astype(BF16)[:, :VIRT], amp_ref[0], 1, 0).astype(BF16)


def copy_whole(in_ref, o_ref):
    o_ref[...] = in_ref[...]


def choose_rows(info, own_ref, a_ref, b_ref, o_ref):
    @pl.when(info[1] == 1)
    def _():
        o_ref[0] = own_ref[...]
        o_ref[1] = a_ref[...]

    @pl.when(info[1] == 0)
    def _():
        o_ref[0] = a_ref[...]
        o_ref[1] = b_ref[...]


def choose_onward(info, first_ref, second_ref, o_ref):
    @pl.when(info[0] == 0)
    def _():
        o_ref[...] = first_ref[...]

    @pl.when(info[0] == 1)
    def _():
        o_ref[...] = second_ref[...]


class Factors:
    def __init__(self, info, step, x_refs, slot, first_col, sems):
        own, near, swapped, far, far_pair = x_refs
        self.info, self.step, self.sems = info, step, sems
        self.slot, self.first_col = slot, first_col
        self.sources = {
            (0, 0): (own.at[0], own.at[1]),
            (0, 1): (own.at[1], own.at[0]),
            (1, 0): (swapped.at[1], swapped.at[0]),
            (1, 1): (near.at[1], near.at[0]),
            (2, 0): (far, far_pair),
            (2, 1): (far_pair, far),
            (3, 0): (near.at[0], near.at[1]),
            (3, 1): (swapped.at[0], swapped.at[1]),
        }

    def copy(self, ref, side):
        to = self.slot.at[:, pl.ds(self.first_col + side * BPAD, BPAD)]
        return pltpu.make_async_copy(ref, to, self.sems.at[side])

    def start(self):
        for (place, core), refs in self.sources.items():

            @pl.when((self.info[4 + self.step] == place) & (self.info[0] == core))
            def _():
                for side in range(2):
                    self.copy(refs[side], side).start()

    def wait(self):
        for side in range(2):
            self.copy(self.sources[2, 0][side], side).wait()


def weigh(h_ref, x, z):
    return (dot(h_ref[...], x, 1, 0) * scaled(z)).astype(BF16)


def early_blocks(info, h0_ref, h1_ref, *refs):
    x_refs, z_refs, back_out = refs[:5], refs[5:8], refs[8]
    xs, zs, xsem, zsem = refs[9:]
    for i in range(3):
        Factors(info, i, x_refs, xs.at[i], 0, xsem.at[i]).start()
        pltpu.make_async_copy(z_refs[i], zs.at[i], zsem.at[i]).start()
    back_out[...] = jnp.zeros_like(back_out)

    def block(i, carry):
        Factors(info, i, x_refs, xs.at[i], 0, xsem.at[i]).wait()
        pltpu.make_async_copy(z_refs[0], zs.at[i], zsem.at[i]).wait()
        for b, h_ref in enumerate((h0_ref, h1_ref)):
            rows = slice(b * BPAD, b * BPAD + BPAD)
            x = xs[i]
            back_out[rows, :] += dot(weigh(h_ref, x, zs[i, b]), x, 1, 1)
        return carry

    lax.fori_loop(0, 3, block, 0)


def window_loads(side, w0_ref, w1_ref, left, sems):
    loads = [
        pltpu.make_async_copy(w_ref.at[side], left.at[:, :, pl.ds(b * BPAD, BPAD)], sems.at[b])
        for b, w_ref in enumerate((w0_ref, w1_ref))
    ]
    for load in loads:
        load.start()
    return loads


def give_half(left_loads, left, back, give_ref):
    for load in left_loads:
        load.wait()
    give_ref[...] = dot(left[...].reshape(8 * WIN, TWO), back, 1, 0).astype(BF16)


def last_block(info, h0_ref, h1_ref, *refs):
    x_refs, z_ref, early_ref, w0_ref, w1_ref = refs[:5], *refs[5:9]
    w_out, xn_out, back_out, give_ref, left, xsem, vsem = refs[9:]
    newest = Factors(info, 3, x_refs, xn_out, 0, xsem)
    newest.start()
    left_loads = window_loads(0, w0_ref, w1_ref, left, vsem)
    newest.wait()
    for b, h_ref in enumerate((h0_ref, h1_ref)):
        w_out[b * BPAD : b * BPAD + BPAD, :] = weigh(h_ref, xn_out[...], z_ref[b])
    part = dot(w_out[...], xn_out[:TWO, :], 1, 1)
    back_out[...] = (early_ref[:, :TWO] + part).astype(BF16)
    give_half(left_loads, left, back_out[...], give_ref)


def second_half(early_ref, newest_ref, xn_ref, w0_ref, w1_ref, back_out, give_ref, left, vsem):
    left_loads = window_loads(0, w0_ref, w1_ref, left, vsem)
    part = dot(newest_ref[...], xn_ref[TWO:, :], 1, 1)
    back_out[...] = (early_ref[:, TWO:] + part).astype(BF16)
    give_half(left_loads, left, back_out[...], give_ref)


def keep_sum(back_ref, w0_ref, w1_ref, got_ref, left, vsem):
    for load in window_loads(1, w0_ref, w1_ref, left, vsem):
        load.wait()
    return dot(left[...].reshape(8 * WIN, TWO), back_ref[...], 1, 0) + got_ref[...].astype(F32)


def keep_x(back_ref, w0_ref, w1_ref, got_ref, own_ref, send_ref, left, vsem):
    total = keep_sum(back_ref, w0_ref, w1_ref, got_ref, left, vsem)
    own_ref[...] = total[: 4 * WIN]
    send_ref[...] = total[4 * WIN :].astype(BF16)


def keep_z(back_ref, w0_ref, w1_ref, got_ref, own_ref, *refs):
    send_refs, left, vsem = refs[:3], refs[3], refs[4]
    total = keep_sum(back_ref, w0_ref, w1_ref, got_ref, left, vsem)
    for dx in range(2):
        for dz in range(4):
            part = total[(4 * dx + dz) * WIN : (4 * dx + dz + 1) * WIN]
            if dz == 0:
                own_ref[dx] = part
            else:
                send_refs[dz - 1][dx] = part.astype(BF16)


def then_z(own_ref, got_ref, out_ref, *send_refs):
    total = own_ref[...] + got_ref[...].astype(F32)
    out_ref[...] = total[:WIN]
    for dz in range(1, 4):
        send_refs[dz - 1][...] = total[dz * WIN : (dz + 1) * WIN].astype(BF16)


def then_x(own_ref, got_1, got_2, got_3, out_ref, send_ref):
    total = own_ref[...] + got_1[...].astype(F32) + got_2[...].astype(F32) + got_3[...].astype(F32)
    out_ref[...] = total[0]
    send_ref[...] = total[1].astype(BF16)


def add_parts(own_ref, *refs):
    o_ref = refs[-1]
    total = own_ref[...]
    for ref in refs[:-1]:
        total = total + ref[...].astype(F32)
    o_ref[...] = total


def finish(numbers, occ_ref, vir_ref, a_ref, b_ref, b1_ref, o_ref, out):
    packed, first_row, first_cell = numbers[0], numbers[1], numbers[2]
    count = occ_ref.shape[1]
    orbital = lax.broadcasted_iota(jnp.int32, (1, count), 1)
    starts = orbital * (2 * count - orbital - 1) // 2
    first_occ = jnp.sum(((starts <= packed) & (orbital > 0)).astype(jnp.int32))
    second_occ = packed - first_occ * (2 * count - first_occ - 1) // 2 + first_occ + 1
    occ = jnp.where(orbital == first_occ, occ_ref[...], 0.0)
    occ = occ + jnp.where(orbital == second_occ, occ_ref[...], 0.0)
    row = lax.broadcasted_iota(jnp.int32, (WIN, VIRT), 0) + first_row
    column = lax.broadcasted_iota(jnp.int32, (WIN, VIRT), 1)
    vir = vir_ref[...]
    vir_rows = jnp.sum(jnp.where(row == column, vir, 0.0), axis=1, keepdims=True)
    vir_rows = jnp.where(row[:, :1] < VIRT, vir_rows, 1.0)
    gaps = vir_rows + vir - jnp.sum(occ, axis=1, keepdims=True)
    out[:, :TWO] = a_ref[...] / gaps[:, :TWO]
    total_b = b_ref[...] + b1_ref[...].astype(F32)
    out[:, TWO:] = total_b[:, : VIRT - TWO] / gaps[:, TWO:]
    rows = o_ref.shape[0]
    for shift in range(0, VIRT, BLK):

        @pl.when(first_cell == shift)
        def _():
            if shift == 0:
                o_ref[...] = out[:rows, :]
            else:
                o_ref[:, : VIRT - shift] = out[:rows, shift:]
                o_ref[:, VIRT - shift :] = out[1 : rows + 1, :shift]


def shape(*dims, dtype=BF16):
    return jax.ShapeDtypeStruct(dims, dtype)


def local(amplitudes, factors, z_values, z_scales, pair_index, vir_energy, occ_energy):
    grid_pos = lax.axis_index("grid")
    pair_pos = lax.axis_index("pair")
    z_pos = grid_pos // 4
    x_hi = (grid_pos // 2) % 2
    core = grid_pos % 2
    y_pos = pair_pos // 2
    x_pos = 2 * x_hi + pair_pos % 2
    outer = (x_pos == 0) | (x_pos == 3)
    order = [(y_pos + i - z_pos) % 4 for i in (0, 1, 3, 2)]
    places = [(chip // 2 - z_pos) % 4 + 4 * ((chip % 2 - x_hi) % 2) for chip in range(8)]
    info = jnp.stack([core, outer.astype(jnp.int32), 1 - core, core] + order + places).astype(jnp.int32)

    theirs = across(factors)
    z_own = call(
        pad_metric,
        shape(BPAD, TWO),
        [
            pltpu.VMEM((16, TWO), F32),
            pltpu.VMEM((BLK, 2 * BLK), BF16),
            pltpu.SemaphoreType.DMA,
        ],
        z_values,
        z_scales,
        in_specs=[HBM, SMEM],
        mib=60,
    )
    hop_a = {0: 1, 3: 2, 2: 0, 1: 3}
    hop_b = {2: 1, 1: 2}
    recv_a = move(z_own, lambda z, x, c, y: (z, hop_a[x], c, y))
    recv_b = move(z_own, lambda z, x, c, y: (z, hop_b[x], c, y) if x in hop_b else None)
    theirs, z_own = lax.optimization_barrier((theirs, z_own))
    x_pair, x_own = call(
        pad_factors, (shape(2, VPAD, BPAD), shape(VPAD, BPAD)), [], factors, theirs
    )

    def halves_of(block, amp, weight=0):
        return call(
            half,
            (shape(BPAD, VPAD), shape(2, 8, WIN, BPAD)),
            [pltpu.VMEM((VPAD, BPAD), F32)],
            info,
            block,
            amp,
            in_specs=[SMEM, VMEM, VMEM],
            weight=weight,
        )

    half_0, wins_0 = halves_of(x_own, amplitudes)
    onward = lambda z, x, c, y: (z + 1 - 2 * c, x, c, y)
    near = move(x_pair, onward)
    recv_a, recv_b, half_0, x_again = lax.optimization_barrier((recv_a, recv_b, half_0, x_own))
    x_other = move(x_again, lambda z, x, c, y: (z, 3 - x, c, y))
    z_here = call(
        choose_rows,
        shape(2, BPAD, TWO),
        [],
        info,
        z_own,
        recv_a,
        recv_b,
        in_specs=[SMEM] + [VMEM] * 3,
        weight=8,
    )
    z_before = move(z_here, lambda z, x, c, y: (z, x, c, y + 1))
    z_after = move(z_here, lambda z, x, c, y: (z, x, c, y - 1))
    far = move(near[0], onward)
    amp_later, far_source = lax.optimization_barrier((amplitudes, near))
    amp_again = call(copy_whole, shape(1, VIRT, VIRT), [], amp_later)
    x_other, amp_again = lax.optimization_barrier((x_other, amp_again))
    half_1, wins_1 = halves_of(x_other, amp_again, 10)
    z_before, z_after, half_1 = lax.optimization_barrier((z_before, z_after, half_1))
    z_onward = call(
        choose_onward,
        shape(2, BPAD, TWO),
        [],
        info,
        z_before,
        z_after,
        in_specs=[SMEM] + [VMEM] * 2,
    )
    z_far = move(z_onward, lambda z, x, c, y: (z, x, c, y + 1 - 2 * c))
    x_parts = [x_pair, near, across(near), far, across(far)]
    dma = pltpu.SemaphoreType.DMA
    early = call(
        early_blocks,
        shape(TWO, VPAD, dtype=F32),
        [
            pltpu.VMEM((3, VPAD, TWO), BF16),
            pltpu.VMEM((3, 2, BPAD, TWO), BF16),
            dma((3, 2)),
            dma((3,)),
        ],
        info,
        half_0,
        half_1,
        *x_parts,
        z_here,
        z_after,
        z_before,
        in_specs=[SMEM] + [VMEM] * 2 + [HBM] * 8,
        mib=20,
    )
    left = pltpu.VMEM((8, WIN, TWO), BF16)
    half_shape = shape(TWO, TWO)
    newest, x_newest, back_a, give_a = call(
        last_block,
        (half_shape, shape(VPAD, TWO), half_shape, half_shape),
        [left, dma((2,)), dma((2,))],
        info,
        half_0,
        half_1,
        *x_parts,
        z_far,
        early,
        wins_0,
        wins_1,
        in_specs=[SMEM] + [VMEM] * 2 + [HBM] * 5 + [VMEM] * 2 + [HBM] * 2,
    )
    got_a = across(give_a)
    back_b, give_b = call(
        second_half,
        (half_shape, half_shape),
        [left, dma((2,))],
        early,
        newest,
        x_newest,
        wins_0,
        wins_1,
        in_specs=[VMEM] * 3 + [HBM] * 2,
    )
    got_b = across(give_b)

    to_z = [None] + [(lambda dz: lambda z, x, c, y: (z + dz, x, c, y))(dz) for dz in range(1, 4)]
    to_x = lambda z, x, c, y: (z, x + 2, c, y)
    own_a, send_a = call(
        keep_x,
        (shape(4 * WIN, TWO, dtype=F32), shape(4 * WIN, TWO)),
        [left, dma((2,))],
        back_a,
        wins_0,
        wins_1,
        got_a,
        in_specs=[VMEM, HBM, HBM, VMEM],
    )
    from_x = move(send_a, to_x)
    own_b, *sends_b = call(
        keep_z,
        tuple([shape(2, WIN, TWO, dtype=F32)] + [shape(2, WIN, TWO)] * 3),
        [left, dma((2,))],
        back_b,
        wins_0,
        wins_1,
        got_b,
        in_specs=[VMEM, HBM, HBM, VMEM],
    )
    from_z = [move(send, to_z[dz]) for dz, send in enumerate(sends_b, start=1)]
    total_a, *sends_a = call(
        then_z, tuple([shape(WIN, TWO, dtype=F32)] + [shape(WIN, TWO)] * 3), [], own_a, from_x
    )
    last_z = [move(send, to_z[dz]) for dz, send in enumerate(sends_a, start=1)]
    total_a, from_z = lax.optimization_barrier((total_a, from_z))
    total_b, send_b = call(
        then_x, (shape(WIN, TWO, dtype=F32), shape(WIN, TWO)), [], own_b, *from_z
    )
    total_a = call(add_parts, shape(WIN, TWO, dtype=F32), [], total_a, *last_z, weight=10)
    share = VIRT * VIRT // 16
    first_row = grid_pos * BLK // 4
    first_cell = grid_pos * share - first_row * VIRT
    numbers = jnp.stack([pair_index[0], first_row, first_cell]).astype(jnp.int32)
    out = call(
        finish,
        shape(94, VIRT, dtype=F32),
        [pltpu.VMEM((WIN, VIRT), F32)],
        numbers,
        occ_energy.reshape(1, -1),
        vir_energy.reshape(1, -1),
        total_a,
        total_b,
        move(send_b, to_x),
        in_specs=[SMEM] + [VMEM] * 5,
    )
    return out.reshape(1, 94 * VIRT)[:, :share]


def solution(mesh):
    placed = (
        P("pair", None, None),
        P(None, "grid"),
        P("grid", "pair"),
        P("grid", "pair"),
        P("pair"),
        P(),
        P(),
    )
    return jax.shard_map(
        local, mesh=mesh, in_specs=placed, out_specs=P("pair", "grid"), check_vma=False
    )
```

```python
import itertools

import jax
import jax.numpy as jnp
from jax import lax
from jax.experimental import pallas as pl
from jax.experimental.pallas import tpu as pltpu
from jax.sharding import PartitionSpec as P

VIRT = 1500
ZBLK = 125
BLK = 375
BPAD = 384
TWO = 2 * BPAD
VPAD = 1536
WIN = 96
BOTH = ("grid", "pair")
ALL = list(itertools.product(range(4), range(4), range(2), range(4)))
F32 = jnp.float32
BF16 = jnp.bfloat16


def flat_index(z, x, c, y):
    return ((z % 4) * 4 + (x % 4) // 2 * 2 + c % 2) * 8 + (y % 4) * 2 + (x % 4) % 2


def move(block, target):
    pairs = []
    for z, x, c, y in ALL:
        dest = target(z, x, c, y)
        if dest is not None:
            pairs.append((flat_index(z, x, c, y), flat_index(*dest)))
    return lax.ppermute(block, BOTH, pairs)


def across(block):
    return move(block, lambda z, x, c, y: (z, x, 1 - c, y))


def dot(a, b, contract_a, contract_b):
    return lax.dot_general(
        a, b, (((contract_a,), (contract_b,)), ((), ())), preferred_element_type=F32
    )


VMEM = pl.BlockSpec(memory_space=pltpu.VMEM)
SMEM = pl.BlockSpec(memory_space=pltpu.SMEM)
HBM = pl.BlockSpec(memory_space=pl.ANY)


def call(kernel, out_shape, scratch, *args, in_specs=None, out_specs=None, mib=12, weight=0):
    many = isinstance(out_shape, (tuple, list))
    return pl.pallas_call(
        kernel,
        out_shape=out_shape,
        in_specs=in_specs or [VMEM] * len(args),
        out_specs=out_specs or (tuple([VMEM] * len(out_shape)) if many else VMEM),
        scratch_shapes=scratch,
        cost_estimate=pl.CostEstimate(flops=1 + weight * 10**9, bytes_accessed=1 + weight * 10**6, transcendentals=0),
        compiler_params=pltpu.CompilerParams(vmem_limit_bytes=mib * 2**20),
    )(*args)


def pad_metric(z_hbm, s_ref, z_out, tail, z_ref, sem):
    load = pltpu.make_async_copy(z_hbm, z_ref, sem)
    load.start()
    tail[...] = jnp.zeros_like(tail)
    lane = lax.broadcasted_iota(jnp.int32, (1, TWO), 1)
    for r in range(3):
        row = jnp.zeros((1, TWO), F32)
        for q in range(6):
            start = (q // 3) * BPAD + (q % 3) * ZBLK
            row = jnp.where((lane >= start) & (lane < start + ZBLK), s_ref[r, q], row)
        for part in range(3):
            piece = row.astype(BF16).astype(F32)
            tail[7 + 3 * part + r : 8 + 3 * part + r, :] = piece
            row = row - piece
    load.wait()
    top = BPAD - 16
    for half in range(2):
        cols = slice(half * BLK, half * BLK + BLK)
        z_out[:, half * BPAD + 256 : half * BPAD + BPAD] = jnp.zeros((BPAD, 128), BF16)
        z_out[:top, half * BPAD : half * BPAD + BLK] = z_ref[:top, cols]
        tail[:7, half * BPAD : half * BPAD + BLK] = z_ref[top:, cols].astype(F32)
    z_out[top:, :] = tail[...].astype(BF16)


def pad_factors(own_ref, pair_ref, both_out, own_out):
    for out, ref in ((both_out.at[0], own_ref), (both_out.at[1], pair_ref), (own_out, own_ref)):
        out[:, 256:] = jnp.zeros((VPAD, BPAD - 256), BF16)
        out[VIRT - 12 :, :] = jnp.zeros((VPAD - VIRT + 12, BPAD), BF16)
        out[:VIRT, :BLK] = ref[...]


def scaled(block):
    z = block.astype(F32)
    tail = z[BPAD - 16 :, :]
    parts = [tail[7 + r : 8 + r] + tail[10 + r : 11 + r] + tail[13 + r : 14 + r] for r in range(3)]
    row = lax.broadcasted_iota(jnp.int32, (BPAD, 1), 0)
    scale = jnp.where(row < ZBLK, parts[0], jnp.where(row < 2 * ZBLK, parts[1], parts[2]))
    return jnp.where(row < BLK, z * scale, 0.0)


def half(info, x_ref, amp_ref, h_ref, w_ref, xf):
    if x_ref.shape != xf.shape:
        xf[...] = jnp.zeros_like(xf)
    xf[: x_ref.shape[0], : x_ref.shape[1]] = x_ref[...].astype(F32)
    for c in range(2):
        for chip in range(8):
            start = (chip * 2 + c) * BLK // 4
            w_ref[info[2 + c], info[8 + chip]] = xf[start : start + WIN, :].astype(BF16)
    h_ref[...] = jnp.zeros_like(h_ref)
    h_ref[:, :VIRT] = dot(xf[...].T.astype(BF16)[:, :VIRT], amp_ref[0], 1, 0).astype(BF16)


def copy_whole(in_ref, o_ref):
    o_ref[...] = in_ref[...]


def choose_rows(info, own_ref, a_ref, b_ref, o_ref):
    @pl.when(info[1] == 1)
    def _():
        o_ref[0] = own_ref[...]
        o_ref[1] = a_ref[...]

    @pl.when(info[1] == 0)
    def _():
        o_ref[0] = a_ref[...]
        o_ref[1] = b_ref[...]


def choose_onward(info, first_ref, second_ref, o_ref):
    @pl.when(info[0] == 0)
    def _():
        o_ref[...] = first_ref[...]

    @pl.when(info[0] == 1)
    def _():
        o_ref[...] = second_ref[...]


class Factors:
    def __init__(self, info, step, x_refs, slot, first_col, sems):
        own, near, swapped, far, far_pair = x_refs
        self.info, self.step, self.sems = info, step, sems
        self.slot, self.first_col = slot, first_col
        self.sources = {
            (0, 0): (own.at[0], own.at[1]),
            (0, 1): (own.at[1], own.at[0]),
            (1, 0): (swapped.at[1], swapped.at[0]),
            (1, 1): (near.at[1], near.at[0]),
            (2, 0): (far, far_pair),
            (2, 1): (far_pair, far),
            (3, 0): (near.at[0], near.at[1]),
            (3, 1): (swapped.at[0], swapped.at[1]),
        }

    def copy(self, ref, side):
        to = self.slot.at[:, pl.ds(self.first_col + side * BPAD, BPAD)]
        return pltpu.make_async_copy(ref, to, self.sems.at[side])

    def start(self):
        for (place, core), refs in self.sources.items():

            @pl.when((self.info[4 + self.step] == place) & (self.info[0] == core))
            def _():
                for side in range(2):
                    self.copy(refs[side], side).start()

    def wait(self):
        for side in range(2):
            self.copy(self.sources[2, 0][side], side).wait()


def weigh(h_ref, x, z):
    return (dot(h_ref[...], x, 1, 0) * scaled(z)).astype(BF16)


def early_blocks(info, h0_ref, h1_ref, *refs):
    x_refs, z_refs, back_out = refs[:5], refs[5:8], refs[8]
    xs, zs, xsem, zsem = refs[9:]
    for i in range(3):
        Factors(info, i, x_refs, xs.at[i], 0, xsem.at[i]).start()
        pltpu.make_async_copy(z_refs[i], zs.at[i], zsem.at[i]).start()
    back_out[...] = jnp.zeros_like(back_out)

    def block(i, carry):
        Factors(info, i, x_refs, xs.at[i], 0, xsem.at[i]).wait()
        pltpu.make_async_copy(z_refs[0], zs.at[i], zsem.at[i]).wait()
        for b, h_ref in enumerate((h0_ref, h1_ref)):
            rows = slice(b * BPAD, b * BPAD + BPAD)
            x = xs[i]
            back_out[rows, :] += dot(weigh(h_ref, x, zs[i, b]), x, 1, 1)
        return carry

    lax.fori_loop(0, 3, block, 0)


def window_loads(side, w0_ref, w1_ref, left, sems):
    loads = [
        pltpu.make_async_copy(w_ref.at[side], left.at[:, :, pl.ds(b * BPAD, BPAD)], sems.at[b])
        for b, w_ref in enumerate((w0_ref, w1_ref))
    ]
    for load in loads:
        load.start()
    return loads


def give_half(left_loads, left, back, give_ref):
    for load in left_loads:
        load.wait()
    give_ref[...] = dot(left[...].reshape(8 * WIN, TWO), back, 1, 0).astype(BF16)


def last_block(info, h0_ref, h1_ref, *refs):
    x_refs, z_ref, early_ref, w0_ref, w1_ref = refs[:5], *refs[5:9]
    w_out, xn_out, back_out, give_ref, left, xsem, vsem = refs[9:]
    newest = Factors(info, 3, x_refs, xn_out, 0, xsem)
    newest.start()
    left_loads = window_loads(0, w0_ref, w1_ref, left, vsem)
    newest.wait()
    for b, h_ref in enumerate((h0_ref, h1_ref)):
        w_out[b * BPAD : b * BPAD + BPAD, :] = weigh(h_ref, xn_out[...], z_ref[b])
    part = dot(w_out[...], xn_out[:TWO, :], 1, 1)
    back_out[...] = (early_ref[:, :TWO] + part).astype(BF16)
    give_half(left_loads, left, back_out[...], give_ref)


def second_half(early_ref, newest_ref, xn_ref, w0_ref, w1_ref, back_out, give_ref, left, vsem):
    left_loads = window_loads(0, w0_ref, w1_ref, left, vsem)
    part = dot(newest_ref[...], xn_ref[TWO:, :], 1, 1)
    back_out[...] = (early_ref[:, TWO:] + part).astype(BF16)
    give_half(left_loads, left, back_out[...], give_ref)


def keep_sum(back_ref, w0_ref, w1_ref, got_ref, left, vsem):
    for load in window_loads(1, w0_ref, w1_ref, left, vsem):
        load.wait()
    return dot(left[...].reshape(8 * WIN, TWO), back_ref[...], 1, 0) + got_ref[...].astype(F32)


def keep_x(back_ref, w0_ref, w1_ref, got_ref, own_ref, send_ref, left, vsem):
    total = keep_sum(back_ref, w0_ref, w1_ref, got_ref, left, vsem)
    own_ref[...] = total[: 4 * WIN]
    send_ref[...] = total[4 * WIN :].astype(BF16)


def keep_z(back_ref, w0_ref, w1_ref, got_ref, own_ref, *refs):
    send_refs, left, vsem = refs[:3], refs[3], refs[4]
    total = keep_sum(back_ref, w0_ref, w1_ref, got_ref, left, vsem)
    for dx in range(2):
        for dz in range(4):
            part = total[(4 * dx + dz) * WIN : (4 * dx + dz + 1) * WIN]
            if dz == 0:
                own_ref[dx] = part
            else:
                send_refs[dz - 1][dx] = part.astype(BF16)


def then_z(own_ref, got_ref, out_ref, *send_refs):
    total = own_ref[...] + got_ref[...].astype(F32)
    out_ref[...] = total[:WIN]
    for dz in range(1, 4):
        send_refs[dz - 1][...] = total[dz * WIN : (dz + 1) * WIN].astype(BF16)


def then_x(own_ref, got_1, got_2, got_3, out_ref, send_ref):
    total = own_ref[...] + got_1[...].astype(F32) + got_2[...].astype(F32) + got_3[...].astype(F32)
    out_ref[...] = total[0]
    send_ref[...] = total[1].astype(BF16)


def add_parts(own_ref, *refs):
    o_ref = refs[-1]
    total = own_ref[...]
    for ref in refs[:-1]:
        total = total + ref[...].astype(F32)
    o_ref[...] = total


def finish(numbers, occ_ref, vir_ref, a_ref, b_ref, b1_ref, o_ref, out):
    packed, first_row, first_cell = numbers[0], numbers[1], numbers[2]
    count = occ_ref.shape[1]
    orbital = lax.broadcasted_iota(jnp.int32, (1, count), 1)
    starts = orbital * (2 * count - orbital - 1) // 2
    first_occ = jnp.sum(((starts <= packed) & (orbital > 0)).astype(jnp.int32))
    second_occ = packed - first_occ * (2 * count - first_occ - 1) // 2 + first_occ + 1
    occ = jnp.where(orbital == first_occ, occ_ref[...], 0.0)
    occ = occ + jnp.where(orbital == second_occ, occ_ref[...], 0.0)
    row = lax.broadcasted_iota(jnp.int32, (WIN, VIRT), 0) + first_row
    column = lax.broadcasted_iota(jnp.int32, (WIN, VIRT), 1)
    vir = vir_ref[...]
    vir_rows = jnp.sum(jnp.where(row == column, vir, 0.0), axis=1, keepdims=True)
    vir_rows = jnp.where(row[:, :1] < VIRT, vir_rows, 1.0)
    gaps = vir_rows + vir - jnp.sum(occ, axis=1, keepdims=True)
    out[:, :TWO] = a_ref[...] / gaps[:, :TWO]
    total_b = b_ref[...] + b1_ref[...].astype(F32)
    out[:, TWO:] = total_b[:, : VIRT - TWO] / gaps[:, TWO:]
    rows = o_ref.shape[0]
    for shift in range(0, VIRT, BLK):

        @pl.when(first_cell == shift)
        def _():
            if shift == 0:
                o_ref[...] = out[:rows, :]
            else:
                o_ref[:, : VIRT - shift] = out[:rows, shift:]
                o_ref[:, VIRT - shift :] = out[1 : rows + 1, :shift]


def shape(*dims, dtype=BF16):
    return jax.ShapeDtypeStruct(dims, dtype)


def local(amplitudes, factors, z_values, z_scales, pair_index, vir_energy, occ_energy):
    grid_pos = lax.axis_index("grid")
    pair_pos = lax.axis_index("pair")
    z_pos = grid_pos // 4
    x_hi = (grid_pos // 2) % 2
    core = grid_pos % 2
    y_pos = pair_pos // 2
    x_pos = 2 * x_hi + pair_pos % 2
    outer = (x_pos == 0) | (x_pos == 3)
    order = [(y_pos + i - z_pos) % 4 for i in (0, 1, 3, 2)]
    places = [(chip // 2 - z_pos) % 4 + 4 * ((chip % 2 - x_hi) % 2) for chip in range(8)]
    info = jnp.stack([core, outer.astype(jnp.int32), 1 - core, core] + order + places).astype(jnp.int32)

    theirs = across(factors)
    z_own = call(
        pad_metric,
        shape(BPAD, TWO),
        [
            pltpu.VMEM((16, TWO), F32),
            pltpu.VMEM((BLK, 2 * BLK), BF16),
            pltpu.SemaphoreType.DMA,
        ],
        z_values,
        z_scales,
        in_specs=[HBM, SMEM],
        mib=60,
    )
    hop_a = {0: 1, 3: 2, 2: 0, 1: 3}
    hop_b = {2: 1, 1: 2}
    recv_a = move(z_own, lambda z, x, c, y: (z, hop_a[x], c, y))
    recv_b = move(z_own, lambda z, x, c, y: (z, hop_b[x], c, y) if x in hop_b else None)
    theirs, z_own = lax.optimization_barrier((theirs, z_own))
    x_pair, x_own = call(
        pad_factors, (shape(2, VPAD, BPAD), shape(VPAD, BPAD)), [], factors, theirs
    )

    def halves_of(block, amp, weight=0):
        return call(
            half,
            (shape(BPAD, VPAD), shape(2, 8, WIN, BPAD)),
            [pltpu.VMEM((VPAD, BPAD), F32)],
            info,
            block,
            amp,
            in_specs=[SMEM, VMEM, VMEM],
            weight=weight,
        )

    half_0, wins_0 = halves_of(x_own, amplitudes)
    onward = lambda z, x, c, y: (z + 1 - 2 * c, x, c, y)
    near = move(x_pair, onward)
    recv_a, recv_b, half_0, x_again = lax.optimization_barrier((recv_a, recv_b, half_0, x_own))
    x_other = move(x_again, lambda z, x, c, y: (z, 3 - x, c, y))
    z_here = call(
        choose_rows,
        shape(2, BPAD, TWO),
        [],
        info,
        z_own,
        recv_a,
        recv_b,
        in_specs=[SMEM] + [VMEM] * 3,
        weight=8,
    )
    z_before = move(z_here, lambda z, x, c, y: (z, x, c, y + 1))
    z_after = move(z_here, lambda z, x, c, y: (z, x, c, y - 1))
    far = move(near[0], onward)
    amp_later, far_source = lax.optimization_barrier((amplitudes, near))
    amp_again = call(copy_whole, shape(1, VIRT, VIRT), [], amp_later)
    x_other, amp_again = lax.optimization_barrier((x_other, amp_again))
    half_1, wins_1 = halves_of(x_other, amp_again, 10)
    z_before, z_after, half_1 = lax.optimization_barrier((z_before, z_after, half_1))
    z_onward = call(
        choose_onward,
        shape(2, BPAD, TWO),
        [],
        info,
        z_before,
        z_after,
        in_specs=[SMEM] + [VMEM] * 2,
    )
    z_far = move(z_onward, lambda z, x, c, y: (z, x, c, y + 1 - 2 * c))
    x_parts = [x_pair, near, across(near), far, across(far)]
    dma = pltpu.SemaphoreType.DMA
    early = call(
        early_blocks,
        shape(TWO, VPAD, dtype=F32),
        [
            pltpu.VMEM((3, VPAD, TWO), BF16),
            pltpu.VMEM((3, 2, BPAD, TWO), BF16),
            dma((3, 2)),
            dma((3,)),
        ],
        info,
        half_0,
        half_1,
        *x_parts,
        z_here,
        z_after,
        z_before,
        in_specs=[SMEM] + [VMEM] * 2 + [HBM] * 8,
        mib=20,
    )
    left = pltpu.VMEM((8, WIN, TWO), BF16)
    half_shape = shape(TWO, TWO)
    newest, x_newest, back_a, give_a = call(
        last_block,
        (half_shape, shape(VPAD, TWO), half_shape, half_shape),
        [left, dma((2,)), dma((2,))],
        info,
        half_0,
        half_1,
        *x_parts,
        z_far,
        early,
        wins_0,
        wins_1,
        in_specs=[SMEM] + [VMEM] * 2 + [HBM] * 5 + [VMEM] * 2 + [HBM] * 2,
    )
    got_a = across(give_a)
    back_b, give_b = call(
        second_half,
        (half_shape, half_shape),
        [left, dma((2,))],
        early,
        newest,
        x_newest,
        wins_0,
        wins_1,
        in_specs=[VMEM] * 3 + [HBM] * 2,
    )
    got_b = across(give_b)

    to_z = [None] + [(lambda dz: lambda z, x, c, y: (z + dz, x, c, y))(dz) for dz in range(1, 4)]
    to_x = lambda z, x, c, y: (z, x + 2, c, y)
    own_a, send_a = call(
        keep_x,
        (shape(4 * WIN, TWO, dtype=F32), shape(4 * WIN, TWO)),
        [left, dma((2,))],
        back_a,
        wins_0,
        wins_1,
        got_a,
        in_specs=[VMEM, HBM, HBM, VMEM],
    )
    from_x = move(send_a, to_x)
    own_b, *sends_b = call(
        keep_z,
        tuple([shape(2, WIN, TWO, dtype=F32)] + [shape(2, WIN, TWO)] * 3),
        [left, dma((2,))],
        back_b,
        wins_0,
        wins_1,
        got_b,
        in_specs=[VMEM, HBM, HBM, VMEM],
    )
    from_z = [move(sends_b[dz - 1], to_z[dz]) for dz in (2, 1, 3)]
    total_a, *sends_a = call(
        then_z, tuple([shape(WIN, TWO, dtype=F32)] + [shape(WIN, TWO)] * 3), [], own_a, from_x
    )
    last_z = [move(sends_a[dz - 1], to_z[dz]) for dz in (2, 1, 3)]
    total_a, from_z = lax.optimization_barrier((total_a, from_z))
    total_b, send_b = call(
        then_x, (shape(WIN, TWO, dtype=F32), shape(WIN, TWO)), [], own_b, *from_z
    )
    total_a = call(add_parts, shape(WIN, TWO, dtype=F32), [], total_a, *last_z, weight=10)
    share = VIRT * VIRT // 16
    first_row = grid_pos * BLK // 4
    first_cell = grid_pos * share - first_row * VIRT
    numbers = jnp.stack([pair_index[0], first_row, first_cell]).astype(jnp.int32)
    out = call(
        finish,
        shape(94, VIRT, dtype=F32),
        [pltpu.VMEM((WIN, VIRT), F32)],
        numbers,
        occ_energy.reshape(1, -1),
        vir_energy.reshape(1, -1),
        total_a,
        total_b,
        move(send_b, to_x),
        in_specs=[SMEM] + [VMEM] * 5,
    )
    return out.reshape(1, 94 * VIRT)[:, :share]


def solution(mesh):
    placed = (
        P("pair", None, None),
        P(None, "grid"),
        P("grid", "pair"),
        P("grid", "pair"),
        P("pair"),
        P(),
        P(),
    )
    return jax.shard_map(
        local, mesh=mesh, in_specs=placed, out_specs=P("pair", "grid"), check_vma=False
    )
```

```python
import itertools

import jax
import jax.numpy as jnp
from jax import lax
from jax.experimental import pallas as pl
from jax.experimental.pallas import tpu as pltpu
from jax.sharding import PartitionSpec as P

VIRT = 1500
ZBLK = 125
BLK = 375
BPAD = 384
TWO = 2 * BPAD
VPAD = 1536
WIN = 96
BOTH = ("grid", "pair")
ALL = list(itertools.product(range(4), range(4), range(2), range(4)))
F32 = jnp.float32
BF16 = jnp.bfloat16


def flat_index(z, x, c, y):
    return ((z % 4) * 4 + (x % 4) // 2 * 2 + c % 2) * 8 + (y % 4) * 2 + (x % 4) % 2


def move(block, target):
    pairs = []
    for z, x, c, y in ALL:
        dest = target(z, x, c, y)
        if dest is not None:
            pairs.append((flat_index(z, x, c, y), flat_index(*dest)))
    return lax.ppermute(block, BOTH, pairs)


def across(block):
    return move(block, lambda z, x, c, y: (z, x, 1 - c, y))


def dot(a, b, contract_a, contract_b):
    return lax.dot_general(
        a, b, (((contract_a,), (contract_b,)), ((), ())), preferred_element_type=F32
    )


VMEM = pl.BlockSpec(memory_space=pltpu.VMEM)
SMEM = pl.BlockSpec(memory_space=pltpu.SMEM)
HBM = pl.BlockSpec(memory_space=pl.ANY)


def call(kernel, out_shape, scratch, *args, in_specs=None, out_specs=None, mib=12, weight=0):
    many = isinstance(out_shape, (tuple, list))
    return pl.pallas_call(
        kernel,
        out_shape=out_shape,
        in_specs=in_specs or [VMEM] * len(args),
        out_specs=out_specs or (tuple([VMEM] * len(out_shape)) if many else VMEM),
        scratch_shapes=scratch,
        cost_estimate=pl.CostEstimate(flops=1 + weight * 10**9, bytes_accessed=1 + weight * 10**6, transcendentals=0),
        compiler_params=pltpu.CompilerParams(vmem_limit_bytes=mib * 2**20),
    )(*args)


def pad_metric(z_hbm, s_ref, z_out, tail, z_ref, sem):
    load = pltpu.make_async_copy(z_hbm, z_ref, sem)
    load.start()
    tail[...] = jnp.zeros_like(tail)
    lane = lax.broadcasted_iota(jnp.int32, (1, TWO), 1)
    for r in range(3):
        row = jnp.zeros((1, TWO), F32)
        for q in range(6):
            start = (q // 3) * BPAD + (q % 3) * ZBLK
            row = jnp.where((lane >= start) & (lane < start + ZBLK), s_ref[r, q], row)
        for part in range(3):
            piece = row.astype(BF16).astype(F32)
            tail[7 + 3 * part + r : 8 + 3 * part + r, :] = piece
            row = row - piece
    load.wait()
    top = BPAD - 16
    for half in range(2):
        cols = slice(half * BLK, half * BLK + BLK)
        z_out[:, half * BPAD + 256 : half * BPAD + BPAD] = jnp.zeros((BPAD, 128), BF16)
        z_out[:top, half * BPAD : half * BPAD + BLK] = z_ref[:top, cols]
        tail[:7, half * BPAD : half * BPAD + BLK] = z_ref[top:, cols].astype(F32)
    z_out[top:, :] = tail[...].astype(BF16)


def pad_factors(own_ref, pair_ref, both_out, own_out):
    for out, ref in ((both_out.at[0], own_ref), (both_out.at[1], pair_ref), (own_out, own_ref)):
        out[:, 256:] = jnp.zeros((VPAD, BPAD - 256), BF16)
        out[VIRT - 12 :, :] = jnp.zeros((VPAD - VIRT + 12, BPAD), BF16)
        out[:VIRT, :BLK] = ref[...]


def scaled(block):
    z = block.astype(F32)
    tail = z[BPAD - 16 :, :]
    parts = [tail[7 + r : 8 + r] + tail[10 + r : 11 + r] + tail[13 + r : 14 + r] for r in range(3)]
    row = lax.broadcasted_iota(jnp.int32, (BPAD, 1), 0)
    scale = jnp.where(row < ZBLK, parts[0], jnp.where(row < 2 * ZBLK, parts[1], parts[2]))
    return jnp.where(row < BLK, z * scale, 0.0)


def half(info, x_ref, amp_ref, h_ref, w_ref, xf):
    if x_ref.shape != xf.shape:
        xf[...] = jnp.zeros_like(xf)
    xf[: x_ref.shape[0], : x_ref.shape[1]] = x_ref[...].astype(F32)
    for c in range(2):
        for chip in range(8):
            start = (chip * 2 + c) * BLK // 4
            w_ref[info[2 + c], info[8 + chip]] = xf[start : start + WIN, :].astype(BF16)
    h_ref[...] = jnp.zeros_like(h_ref)
    h_ref[:, :VIRT] = dot(xf[...].T.astype(BF16)[:, :VIRT], amp_ref[0], 1, 0).astype(BF16)


def copy_whole(in_ref, o_ref):
    o_ref[...] = in_ref[...]


def choose_rows(info, own_ref, a_ref, b_ref, o_ref):
    @pl.when(info[1] == 1)
    def _():
        o_ref[0] = own_ref[...]
        o_ref[1] = a_ref[...]

    @pl.when(info[1] == 0)
    def _():
        o_ref[0] = a_ref[...]
        o_ref[1] = b_ref[...]


def choose_onward(info, first_ref, second_ref, o_ref):
    @pl.when(info[0] == 0)
    def _():
        o_ref[...] = first_ref[...]

    @pl.when(info[0] == 1)
    def _():
        o_ref[...] = second_ref[...]


class Factors:
    def __init__(self, info, step, x_refs, slot, first_col, sems):
        own, near, swapped, far, far_pair = x_refs
        self.info, self.step, self.sems = info, step, sems
        self.slot, self.first_col = slot, first_col
        self.sources = {
            (0, 0): (own.at[0], own.at[1]),
            (0, 1): (own.at[1], own.at[0]),
            (1, 0): (swapped.at[1], swapped.at[0]),
            (1, 1): (near.at[1], near.at[0]),
            (2, 0): (far, far_pair),
            (2, 1): (far_pair, far),
            (3, 0): (near.at[0], near.at[1]),
            (3, 1): (swapped.at[0], swapped.at[1]),
        }

    def copy(self, ref, side):
        to = self.slot.at[:, pl.ds(self.first_col + side * BPAD, BPAD)]
        return pltpu.make_async_copy(ref, to, self.sems.at[side])

    def start(self):
        for (place, core), refs in self.sources.items():

            @pl.when((self.info[4 + self.step] == place) & (self.info[0] == core))
            def _():
                for side in range(2):
                    self.copy(refs[side], side).start()

    def wait(self):
        for side in range(2):
            self.copy(self.sources[2, 0][side], side).wait()


def weigh(h_ref, x, z):
    return (dot(h_ref[...], x, 1, 0) * scaled(z)).astype(BF16)


def early_blocks(info, h0_ref, h1_ref, *refs):
    x_refs, z_refs, back_out = refs[:5], refs[5:8], refs[8]
    xs, zs, xsem, zsem = refs[9:]
    for i in range(3):
        Factors(info, i, x_refs, xs.at[i], 0, xsem.at[i]).start()
        pltpu.make_async_copy(z_refs[i], zs.at[i], zsem.at[i]).start()
    back_out[...] = jnp.zeros_like(back_out)

    def block(i, carry):
        Factors(info, i, x_refs, xs.at[i], 0, xsem.at[i]).wait()
        pltpu.make_async_copy(z_refs[0], zs.at[i], zsem.at[i]).wait()
        for b, h_ref in enumerate((h0_ref, h1_ref)):
            rows = slice(b * BPAD, b * BPAD + BPAD)
            x = xs[i]
            back_out[rows, :] += dot(weigh(h_ref, x, zs[i, b]), x, 1, 1)
        return carry

    lax.fori_loop(0, 3, block, 0)


def window_loads(side, w0_ref, w1_ref, left, sems):
    loads = [
        pltpu.make_async_copy(w_ref.at[side], left.at[:, :, pl.ds(b * BPAD, BPAD)], sems.at[b])
        for b, w_ref in enumerate((w0_ref, w1_ref))
    ]
    for load in loads:
        load.start()
    return loads


def give_half(left_loads, left, back, give_ref):
    for load in left_loads:
        load.wait()
    give_ref[...] = dot(left[...].reshape(8 * WIN, TWO), back, 1, 0).astype(BF16)


def last_block(info, h0_ref, h1_ref, *refs):
    x_refs, z_ref, early_ref, w0_ref, w1_ref = refs[:5], *refs[5:9]
    w_out, xn_out, back_out, give_ref, keep_ref, left, xsem, vsem, ksem = refs[9:]
    newest = Factors(info, 3, x_refs, xn_out, 0, xsem)
    newest.start()
    left_loads = window_loads(0, w0_ref, w1_ref, left, vsem)
    keep_loads = window_loads(1, w0_ref, w1_ref, keep_ref, ksem)
    newest.wait()
    for b, h_ref in enumerate((h0_ref, h1_ref)):
        w_out[b * BPAD : b * BPAD + BPAD, :] = weigh(h_ref, xn_out[...], z_ref[b])
    part = dot(w_out[...], xn_out[:TWO, :], 1, 1)
    back_out[...] = (early_ref[:, :TWO] + part).astype(BF16)
    give_half(left_loads, left, back_out[...], give_ref)
    for load in keep_loads:
        load.wait()


def second_half(early_ref, newest_ref, xn_ref, w0_ref, w1_ref, back_out, give_ref, left, vsem):
    left_loads = window_loads(0, w0_ref, w1_ref, left, vsem)
    part = dot(newest_ref[...], xn_ref[TWO:, :], 1, 1)
    back_out[...] = (early_ref[:, TWO:] + part).astype(BF16)
    give_half(left_loads, left, back_out[...], give_ref)


def keep_sum(back_ref, left_ref, got_ref):
    left = left_ref[...].reshape(8 * WIN, TWO)
    return dot(left, back_ref[...], 1, 0) + got_ref[...].astype(F32)


def keep_x(back_ref, left_ref, got_ref, own_ref, send_ref):
    total = keep_sum(back_ref, left_ref, got_ref)
    own_ref[...] = total[: 4 * WIN]
    send_ref[...] = total[4 * WIN :].astype(BF16)


def keep_z(back_ref, left_ref, got_ref, own_ref, *send_refs):
    total = keep_sum(back_ref, left_ref, got_ref)
    for dx in range(2):
        for dz in range(4):
            part = total[(4 * dx + dz) * WIN : (4 * dx + dz + 1) * WIN]
            if dz == 0:
                own_ref[dx] = part
            else:
                send_refs[dz - 1][dx] = part.astype(BF16)


def then_z(own_ref, got_ref, out_ref, *send_refs):
    total = own_ref[...] + got_ref[...].astype(F32)
    out_ref[...] = total[:WIN]
    for dz in range(1, 4):
        send_refs[dz - 1][...] = total[dz * WIN : (dz + 1) * WIN].astype(BF16)


def then_x(own_ref, got_1, got_2, got_3, out_ref, send_ref):
    total = own_ref[...] + got_1[...].astype(F32) + got_2[...].astype(F32) + got_3[...].astype(F32)
    out_ref[...] = total[0]
    send_ref[...] = total[1].astype(BF16)


def add_parts(own_ref, *refs):
    o_ref = refs[-1]
    total = own_ref[...]
    for ref in refs[:-1]:
        total = total + ref[...].astype(F32)
    o_ref[...] = total


def finish(numbers, occ_ref, vir_ref, a_ref, b_ref, b1_ref, o_ref, out):
    packed, first_row, first_cell = numbers[0], numbers[1], numbers[2]
    count = occ_ref.shape[1]
    orbital = lax.broadcasted_iota(jnp.int32, (1, count), 1)
    starts = orbital * (2 * count - orbital - 1) // 2
    first_occ = jnp.sum(((starts <= packed) & (orbital > 0)).astype(jnp.int32))
    second_occ = packed - first_occ * (2 * count - first_occ - 1) // 2 + first_occ + 1
    occ = jnp.where(orbital == first_occ, occ_ref[...], 0.0)
    occ = occ + jnp.where(orbital == second_occ, occ_ref[...], 0.0)
    row = lax.broadcasted_iota(jnp.int32, (WIN, VIRT), 0) + first_row
    column = lax.broadcasted_iota(jnp.int32, (WIN, VIRT), 1)
    vir = vir_ref[...]
    vir_rows = jnp.sum(jnp.where(row == column, vir, 0.0), axis=1, keepdims=True)
    vir_rows = jnp.where(row[:, :1] < VIRT, vir_rows, 1.0)
    gaps = vir_rows + vir - jnp.sum(occ, axis=1, keepdims=True)
    out[:, :TWO] = a_ref[...] / gaps[:, :TWO]
    total_b = b_ref[...] + b1_ref[...].astype(F32)
    out[:, TWO:] = total_b[:, : VIRT - TWO] / gaps[:, TWO:]
    rows = o_ref.shape[0]
    for shift in range(0, VIRT, BLK):

        @pl.when(first_cell == shift)
        def _():
            if shift == 0:
                o_ref[...] = out[:rows, :]
            else:
                o_ref[:, : VIRT - shift] = out[:rows, shift:]
                o_ref[:, VIRT - shift :] = out[1 : rows + 1, :shift]


def shape(*dims, dtype=BF16):
    return jax.ShapeDtypeStruct(dims, dtype)


def local(amplitudes, factors, z_values, z_scales, pair_index, vir_energy, occ_energy):
    grid_pos = lax.axis_index("grid")
    pair_pos = lax.axis_index("pair")
    z_pos = grid_pos // 4
    x_hi = (grid_pos // 2) % 2
    core = grid_pos % 2
    y_pos = pair_pos // 2
    x_pos = 2 * x_hi + pair_pos % 2
    outer = (x_pos == 0) | (x_pos == 3)
    order = [(y_pos + i - z_pos) % 4 for i in (0, 1, 3, 2)]
    places = [(chip // 2 - z_pos) % 4 + 4 * ((chip % 2 - x_hi) % 2) for chip in range(8)]
    info = jnp.stack([core, outer.astype(jnp.int32), 1 - core, core] + order + places).astype(jnp.int32)

    theirs = across(factors)
    z_own = call(
        pad_metric,
        shape(BPAD, TWO),
        [
            pltpu.VMEM((16, TWO), F32),
            pltpu.VMEM((BLK, 2 * BLK), BF16),
            pltpu.SemaphoreType.DMA,
        ],
        z_values,
        z_scales,
        in_specs=[HBM, SMEM],
        mib=60,
    )
    hop_a = {0: 1, 3: 2, 2: 0, 1: 3}
    hop_b = {2: 1, 1: 2}
    recv_a = move(z_own, lambda z, x, c, y: (z, hop_a[x], c, y))
    recv_b = move(z_own, lambda z, x, c, y: (z, hop_b[x], c, y) if x in hop_b else None)
    theirs, z_own = lax.optimization_barrier((theirs, z_own))
    x_pair, x_own = call(
        pad_factors, (shape(2, VPAD, BPAD), shape(VPAD, BPAD)), [], factors, theirs
    )

    def halves_of(block, amp, weight=0):
        return call(
            half,
            (shape(BPAD, VPAD), shape(2, 8, WIN, BPAD)),
            [pltpu.VMEM((VPAD, BPAD), F32)],
            info,
            block,
            amp,
            in_specs=[SMEM, VMEM, VMEM],
            weight=weight,
        )

    half_0, wins_0 = halves_of(x_own, amplitudes)
    onward = lambda z, x, c, y: (z + 1 - 2 * c, x, c, y)
    near = move(x_pair, onward)
    recv_a, recv_b, half_0, x_again = lax.optimization_barrier((recv_a, recv_b, half_0, x_own))
    x_other = move(x_again, lambda z, x, c, y: (z, 3 - x, c, y))
    z_here = call(
        choose_rows,
        shape(2, BPAD, TWO),
        [],
        info,
        z_own,
        recv_a,
        recv_b,
        in_specs=[SMEM] + [VMEM] * 3,
        weight=8,
    )
    z_before = move(z_here, lambda z, x, c, y: (z, x, c, y + 1))
    z_after = move(z_here, lambda z, x, c, y: (z, x, c, y - 1))
    far = move(near[0], onward)
    amp_later, far_source = lax.optimization_barrier((amplitudes, near))
    amp_again = call(copy_whole, shape(1, VIRT, VIRT), [], amp_later)
    x_other, amp_again = lax.optimization_barrier((x_other, amp_again))
    half_1, wins_1 = halves_of(x_other, amp_again, 10)
    z_before, z_after, half_1 = lax.optimization_barrier((z_before, z_after, half_1))
    z_onward = call(
        choose_onward,
        shape(2, BPAD, TWO),
        [],
        info,
        z_before,
        z_after,
        in_specs=[SMEM] + [VMEM] * 2,
    )
    z_far = move(z_onward, lambda z, x, c, y: (z, x, c, y + 1 - 2 * c))
    x_parts = [x_pair, near, across(near), far, across(far)]
    dma = pltpu.SemaphoreType.DMA
    early = call(
        early_blocks,
        shape(TWO, VPAD, dtype=F32),
        [
            pltpu.VMEM((3, VPAD, TWO), BF16),
            pltpu.VMEM((3, 2, BPAD, TWO), BF16),
            dma((3, 2)),
            dma((3,)),
        ],
        info,
        half_0,
        half_1,
        *x_parts,
        z_here,
        z_after,
        z_before,
        in_specs=[SMEM] + [VMEM] * 2 + [HBM] * 8,
        mib=20,
    )
    left = pltpu.VMEM((8, WIN, TWO), BF16)
    half_shape = shape(TWO, TWO)
    newest, x_newest, back_a, give_a, kept = call(
        last_block,
        (half_shape, shape(VPAD, TWO), half_shape, half_shape, shape(8, WIN, TWO)),
        [left, dma((2,)), dma((2,)), dma((2,))],
        info,
        half_0,
        half_1,
        *x_parts,
        z_far,
        early,
        wins_0,
        wins_1,
        in_specs=[SMEM] + [VMEM] * 2 + [HBM] * 5 + [VMEM] * 2 + [HBM] * 2,
    )
    got_a = across(give_a)
    back_b, give_b = call(
        second_half,
        (half_shape, half_shape),
        [left, dma((2,))],
        early,
        newest,
        x_newest,
        wins_0,
        wins_1,
        in_specs=[VMEM] * 3 + [HBM] * 2,
    )
    got_b = across(give_b)

    to_z = [None] + [(lambda dz: lambda z, x, c, y: (z + dz, x, c, y))(dz) for dz in range(1, 4)]
    to_x = lambda z, x, c, y: (z, x + 2, c, y)
    own_a, send_a = call(
        keep_x,
        (shape(4 * WIN, TWO, dtype=F32), shape(4 * WIN, TWO)),
        [],
        back_a,
        kept,
        got_a,
    )
    from_x = move(send_a, to_x)
    own_b, *sends_b = call(
        keep_z,
        tuple([shape(2, WIN, TWO, dtype=F32)] + [shape(2, WIN, TWO)] * 3),
        [],
        back_b,
        kept,
        got_b,
    )
    from_z = [move(sends_b[dz - 1], to_z[dz]) for dz in (2, 1, 3)]
    total_a, *sends_a = call(
        then_z, tuple([shape(WIN, TWO, dtype=F32)] + [shape(WIN, TWO)] * 3), [], own_a, from_x
    )
    last_z = [move(sends_a[dz - 1], to_z[dz]) for dz in (2, 1, 3)]
    total_a, from_z = lax.optimization_barrier((total_a, from_z))
    total_b, send_b = call(
        then_x, (shape(WIN, TWO, dtype=F32), shape(WIN, TWO)), [], own_b, *from_z
    )
    total_a = call(add_parts, shape(WIN, TWO, dtype=F32), [], total_a, *last_z, weight=10)
    share = VIRT * VIRT // 16
    first_row = grid_pos * BLK // 4
    first_cell = grid_pos * share - first_row * VIRT
    numbers = jnp.stack([pair_index[0], first_row, first_cell]).astype(jnp.int32)
    out = call(
        finish,
        shape(94, VIRT, dtype=F32),
        [pltpu.VMEM((WIN, VIRT), F32)],
        numbers,
        occ_energy.reshape(1, -1),
        vir_energy.reshape(1, -1),
        total_a,
        total_b,
        move(send_b, to_x),
        in_specs=[SMEM] + [VMEM] * 5,
    )
    return out.reshape(1, 94 * VIRT)[:, :share]


def solution(mesh):
    placed = (
        P("pair", None, None),
        P(None, "grid"),
        P("grid", "pair"),
        P("grid", "pair"),
        P("pair"),
        P(),
        P(),
    )
    return jax.shard_map(
        local, mesh=mesh, in_specs=placed, out_specs=P("pair", "grid"), check_vma=False
    )
```
